512 devices in a mesh: ctx: 64 (over z, y_hi, x), exp: 8 (over y_lo, core).
Axes of the slice: x: 4, y: 8 (y_hi: 2, y_lo: 4; y = y_hi * 4 + y_lo), z: 8, core: 2. Of those that a mesh axis runs over, the one named last changes fastest.
Arguments:
- queries: bfloat16 [2048, 73728], P(('ctx', 'exp')), may hold values from -24 to 24
- latents: bfloat16 [5120, 576], P('ctx'), may hold values from -6 to 6
- offsets: int32 [512], P(('ctx', 'exp')), may hold values from 3072 to 5116, as said below
- moe_input: bfloat16 [256, 5120], P('exp', 'ctx'), may hold values from -6 to 6
- routes: int32 [256, 6], P('exp'), may hold values from 0 to 15, all different within a row; in each aligned block of 32 rows (0 to 31, 32 to 63, ...) at most 16 rows name the same one
- gate_values: float32 [256, 6], P('exp'), may hold values from 0.05 to 0.45
- w_gate: bfloat16 [16, 5120, 1536], P('exp', 'ctx'), may hold values from -0.078125 to 0.078125
- w_up: bfloat16 [16, 5120, 1536], P('exp', 'ctx'), may hold values from -0.078125 to 0.078125
- w_down: bfloat16 [16, 1536, 5120], P('exp', None, 'ctx'), may hold values from -0.15625 to 0.15625
Outputs:
- attention_out: bfloat16 [2048, 65536], P(('ctx', 'exp'))
- moe_output: bfloat16 [256, 5120], P('exp', 'ctx')
The draws below stay inside these ranges and needn't reach their ends.
Inputs may be any that keep to these rules, and one draw needn't show every extreme that they name: `offsets`: the query blocks start at distinct positions 3072 + k * 4, one block for each k. `routes`: each row names 6 different experts; the 32 rows of one index of exp name no expert more than 16 times, and in every draw some expert is named exactly 16 times there.
All inputs are finite; a program needn't handle non-finite values.
Results may differ from the reference program's by a relative error of at most 0.0075.
Values may be sent and summed in bfloat16 or wider, within the bound.
No kernel may reach another device: no remote copies, remote signals or barrier semaphores. Data moves between devices by JAX's collectives and lax.ppermute only.
A program may use at most 64 MiB of HBM per device.

```python
import math
import jax
import jax.numpy as jnp
import numpy as np
from jax import lax

D = 5120
FF = 1536
H = 128
LAT = 512
ROPE = 64
TOPK = 6
EXPERTS = 16
QD = 4
MT = 32
CAP = 16
STRETCH = 2048
CTX = 5120
MTOK = 256


def draw_latents(key, part):
    base_key = jax.random.fold_in(key, 13)
    values = jnp.clip(jax.random.normal(base_key, (CTX, LAT + ROPE), jnp.float32), -6.0, 6.0)
    return values.astype(jnp.bfloat16)


def draw_queries(key, part):
    base_key = jax.random.fold_in(key, 11)
    values = jnp.clip(1.15 * jax.random.normal(base_key, (STRETCH * H, LAT + ROPE), jnp.float32), -6.9, 6.9)
    return values.reshape(STRETCH, H * (LAT + ROPE)).astype(jnp.bfloat16)


def draw_offsets(key, part):
    blocks = STRETCH // QD
    ordering = jax.random.permutation(jax.random.fold_in(key, 17), blocks)
    return (CTX - STRETCH + ordering.astype(jnp.int32) * QD).astype(jnp.int32)


def level_of(key, extent, shards, least, largest):
    gain = 1.0
    for axis_at, shards_of in shards:
        steps = jax.random.uniform(jax.random.fold_in(jax.random.fold_in(key, 6), axis_at), (shards_of,), jnp.float32, least / len(shards), largest / len(shards))
        gain = gain * jnp.repeat(jnp.exp(steps), extent[axis_at] // shards_of).reshape((-1,) + (1,) * (len(extent) - 1 - axis_at))
    return gain


def deal_out(rng, own, number, rows, amount, top, most, lean):
    order = jax.random.permutation(rng, amount)
    heavy_load, ordinary = load_shares(amount, rows * top, most, lean, True), load_shares(amount, rows * top, most, lean, False)
    places = jnp.arange(amount)

    def named(tallies, offset_by):
        used = int((tallies > 0).sum())
        fixed = max(1, used // 4)
        passed = fixed + (places - fixed + offset_by * (used - fixed)) % max(1, amount - fixed)
        return jnp.zeros((amount,), jnp.int32).at[order[jnp.where(places < fixed, places, passed)]].set(jnp.asarray(tallies, jnp.int32))

    tallies = jnp.where(number % 4 == 0, named(heavy_load, number // 4), named(ordinary, number - number // 4 - 1))
    mixed = jax.random.permutation(jax.random.fold_in(own, 3), amount)
    giver, receiver = mixed[0:amount // 2 * 2:2], mixed[1:amount // 2 * 2:2]
    room = jnp.minimum(tallies[giver] - 1, most - tallies[receiver]) // 2
    room = jnp.where((giver == order[0]) | (receiver == order[0]) | (tallies[receiver] == 0), 0, jnp.maximum(room, 0))
    passed = jax.random.randint(jax.random.fold_in(own, 4), (amount // 2,), 0, 1 << 20) % (room + 1)
    tallies = tallies.at[giver].add(-passed).at[receiver].add(passed)
    items = jnp.searchsorted(jnp.cumsum(tallies), jnp.arange(rows * top), side="right").astype(jnp.int32)
    table = items.reshape(top, rows).T
    table = table[jax.random.permutation(jax.random.fold_in(own, 1), rows)]
    offset_by = jax.random.randint(jax.random.fold_in(own, 2), (rows, 1), 0, top)
    return jnp.take_along_axis(table, (jnp.arange(top)[None, :] + offset_by) % top, axis=1)


def load_shares(count, total, bound, skew, full):
    portions = [(1 << 20) // math.isqrt(rank ** skew) + 1 for rank in range(1, count + 1)]
    largest = bound if full else min(bound, max(-(-total // count), total * portions[0] // sum(portions)))
    least = 1 if total - largest >= count - 1 else 0
    counts, spare = [largest] + [least] * (count - 1), total - largest - least * (count - 1)
    while spare > 0:
        candidates = [i for i in range(1, count) if counts[i] < largest] or [i for i in range(1, count) if counts[i] < bound]
        whole, remaining = sum([portions[i] for i in candidates]), spare
        for i in candidates:
            addition = min(bound - counts[i], max(1, remaining * portions[i] // whole), spare)
            counts[i] = counts[i] + addition
            spare = spare - addition
    return np.array(counts)


def centred(rng, dims, scale, most, pieces=(), held_as=jnp.bfloat16):
    drawn = scale * jax.random.normal(rng, dims, jnp.float32)
    if pieces:
        drawn = drawn * level_of(rng, dims, pieces, -0.22, 0.18)
    return jnp.clip(drawn, -most, most).astype(held_as)


def setup_inputs(seed: int = 0) -> dict:
    arg_keys = jax.random.split(jax.random.key(seed), 10)
    queries = draw_queries(jax.random.fold_in(arg_keys[9], 71), 0)
    latents = draw_latents(jax.random.fold_in(arg_keys[9], 71), 0)
    offsets = draw_offsets(jax.random.fold_in(arg_keys[9], 71), 0)
    moe_input = centred(arg_keys[3], (MTOK, D), 1.0, 6.0, ((0, 8), (1, 64)))
    routes_keys = jax.random.split(jax.random.fold_in(arg_keys[4], 1), MTOK // MT)
    routes_turns = jax.random.permutation(jax.random.fold_in(arg_keys[4], 3), MTOK // MT)
    routes = jax.vmap(lambda own, number: deal_out(jax.random.fold_in(arg_keys[4], 2), own, number, MT, EXPERTS, TOPK, CAP, 2))(routes_keys, routes_turns).reshape((MTOK, TOPK))
    gate_values = jnp.clip(0.05 + 0.39999999 * jax.random.uniform(arg_keys[5], (MTOK, TOPK), jnp.float32) ** level_of(arg_keys[5], (MTOK, TOPK), ((0, 8),), -0.2, 0.2), 0.05, 0.45)
    w_gate = centred(arg_keys[6], (EXPERTS, D, FF), D ** -0.5, 0.078125, ((0, 8), (1, 64)))
    w_up = centred(arg_keys[7], (EXPERTS, D, FF), D ** -0.5, 0.078125, ((0, 8), (1, 64)))
    w_down = centred(arg_keys[8], (EXPERTS, FF, D), FF ** -0.5, 0.15625, ((0, 8), (2, 64)))
    return dict(queries=queries, latents=latents, offsets=offsets, moe_input=moe_input, routes=routes, gate_values=gate_values, w_gate=w_gate, w_up=w_up, w_down=w_down)


softmax_scale = 192.0 ** -0.5


def attend_group(query_group, positions, latents, key_pos):
    scores = jnp.dot(query_group, latents.T, preferred_element_type=jnp.float32) * softmax_scale
    scores = jnp.where(key_pos[None, :] <= positions[:, None], scores, -jnp.inf)
    row_max = jnp.max(scores, axis=1, keepdims=True)
    weights = jnp.exp(scores - row_max)
    denominator = jnp.sum(weights, axis=1, keepdims=True)
    rounded = weights.astype(jnp.bfloat16)
    mixed = jnp.dot(rounded, latents[:, :LAT], preferred_element_type=jnp.float32)
    return (mixed / denominator).astype(jnp.bfloat16)


def reference(queries, latents, offsets, moe_input, routes, gate_values, w_gate, w_up, w_down):
    token_ids = jnp.arange(STRETCH, dtype=jnp.int32)
    positions = offsets[token_ids // QD] + token_ids % QD
    key_pos = jnp.arange(CTX, dtype=jnp.int32)
    grouped = queries.reshape(STRETCH // 8, 8 * H, LAT + ROPE)
    pos_rows = jnp.repeat(positions, H).reshape(STRETCH // 8, 8 * H)

    def one_group(inputs):
        return attend_group(inputs[0], inputs[1], latents, key_pos)

    mixed = lax.map(one_group, (grouped, pos_rows))
    attention_out = mixed.reshape(STRETCH, H * LAT)

    def expert_out(expert_index):
        gate_act = jnp.dot(moe_input, w_gate[expert_index], preferred_element_type=jnp.float32)
        up_act = jnp.dot(moe_input, w_up[expert_index], preferred_element_type=jnp.float32)
        hidden = (jax.nn.silu(gate_act) * up_act).astype(jnp.bfloat16)
        return jnp.dot(hidden, w_down[expert_index], preferred_element_type=jnp.float32).astype(jnp.bfloat16)

    all_experts = lax.map(expert_out, jnp.arange(EXPERTS, dtype=jnp.int32))
    picked = all_experts[routes, jnp.arange(MTOK, dtype=jnp.int32)[:, None]]
    moe_output = jnp.sum(picked.astype(jnp.float32) * gate_values[:, :, None], axis=1).astype(jnp.bfloat16)
    return (attention_out, moe_output)
```

```python
import functools
import math

import jax
import jax.numpy as jnp
from jax import lax
from jax.experimental import pallas as pl
from jax.experimental.pallas import tpu as pltpu
from jax.sharding import Mesh, PartitionSpec as P

H = 128
LAT = 512
ROPE = 64
WIDE = LAT + ROPE
TOPK = 6
EXPERTS = 16
CAP = 16
KEYS = 512

SCALE_LOG2 = 192.0 ** (-0.5) * math.log2(math.e)
F32 = jnp.float32
BF16 = jnp.bfloat16


def attention_kernel(off_ref, q_ref, pos_ref, mine_ref, other_ref, out_ref, top_ref, den_ref, acc_ref):
    rows = q_ref.shape[0]
    row_pos = off_ref[0] + lax.broadcasted_iota(jnp.int32, (rows, 1), 0) // H
    top_ref[...] = jnp.full_like(top_ref, -1e30)
    den_ref[...] = jnp.zeros_like(den_ref)
    acc_ref[...] = jnp.zeros_like(acc_ref)

    def step(keys_ref, base, i):
        keys = keys_ref[pl.ds(i * KEYS, KEYS), :]
        key_pos = pos_ref[:, pl.ds(base + i * KEYS, KEYS)]
        half = rows // 2
        for r in range(2):
            at = pl.ds(r * half, half)
            scores = lax.dot_general(
                q_ref[at, :], keys, (((1,), (1,)), ((), ())), preferred_element_type=F32
            )
            allowed = key_pos <= row_pos[r * half : (r + 1) * half]
            scores = jnp.where(allowed, scores * SCALE_LOG2, -jnp.inf)
            old = top_ref[at, :1]
            new = jnp.maximum(old, jnp.max(scores, axis=1, keepdims=True))
            shrink = jnp.exp2(old - new)
            weights = jnp.exp2(scores - new)
            den_ref[at, :1] = den_ref[at, :1] * shrink + jnp.sum(weights, axis=1, keepdims=True)
            top_ref[at, :1] = new
            acc_ref[at, :] = acc_ref[at, :] * shrink + jnp.dot(
                weights.astype(BF16), keys[:, :LAT], preferred_element_type=F32
            )

    count = mine_ref.shape[0] // KEYS

    @pl.loop(0, count)
    def _(i):
        step(mine_ref, 0, i)

    @pl.loop(0, count)
    def _(i):
        step(other_ref, mine_ref.shape[0], i)

    out_ref[...] = (acc_ref[...] / den_ref[:, :1]).astype(BF16)


def attend(offset, query_rows, key_pos, mine, other):
    rows = query_rows.shape[0]
    vmem = pl.BlockSpec(memory_space=pltpu.VMEM)
    return pl.pallas_call(
        attention_kernel,
        out_shape=jax.ShapeDtypeStruct((rows, LAT), BF16),
        in_specs=[pl.BlockSpec(memory_space=pltpu.SMEM)] + [vmem] * 4,
        out_specs=vmem,
        scratch_shapes=[
            pltpu.VMEM((rows, 128), F32),
            pltpu.VMEM((rows, 128), F32),
            pltpu.VMEM((rows, LAT), F32),
        ],
        compiler_params=pltpu.CompilerParams(vmem_limit_bytes=40 * 2**20),
        cost_estimate=pl.CostEstimate(
            flops=2 * rows * 5120 * (WIDE + LAT), bytes_accessed=8 * 2**20, transcendentals=rows * 5120
        ),
        name="attend",
    )(offset, query_rows, key_pos, mine, other)


def exchange(array, axes):
    return lax.all_to_all(array, axes, split_axis=0, concat_axis=0, tiled=False)


def spread(array, axes, count):
    return exchange(jnp.broadcast_to(array[None], (count,) + array.shape), axes)


def ring(axis, size, by):
    return [(i, (i + by) % size) for i in range(size)]


def local(queries, latents, offsets, moe_input, routes, gate_values, w_gate, w_up, w_down):
    nz, nh, nx, nl, nc = (lax.axis_size(a) for a in ("z", "h", "x", "l", "c"))
    core = lax.axis_index("c")
    x_at = lax.axis_index("x")
    deep = nz * nh
    owners = nl * nc
    held = w_gate.shape[0]
    tokens, feats = moe_input.shape
    units = w_gate.shape[2] // nx
    slots = held * CAP

    own = latents.shape[0] // nc
    half = lax.dynamic_slice_in_dim(latents, core * own, own, 0)
    column = spread(half, ("z", "h"), deep)
    column = column.reshape(deep * own, WIDE)

    both = jnp.concatenate(
        [w_gate.reshape(held, feats, nx, units), w_up.reshape(held, feats, nx, units)], axis=3
    )
    both = exchange(both.transpose(2, 0, 1, 3), "x")
    down = w_down.transpose(0, 2, 1).reshape(held, feats, nx, units).transpose(2, 0, 1, 3)
    down = exchange(down, "x")

    one_hot = jnp.any(routes[:, :, None] == lax.iota(jnp.int32, EXPERTS), axis=1)
    before = lax.iota(jnp.int32, tokens)[None, :] < lax.iota(jnp.int32, tokens)[:, None]
    rank = jnp.dot(before.astype(BF16), one_hot.astype(BF16), preferred_element_type=F32).astype(jnp.int32)
    placed = one_hot[:, :, None] & (rank[:, :, None] == lax.iota(jnp.int32, CAP))
    placed = placed.reshape(tokens, EXPERTS * CAP)
    outgoing = lax.dot_general(
        placed.astype(BF16), moe_input, (((0,), (0,)), ((), ())), preferred_element_type=F32
    ).astype(BF16)
    outgoing = jnp.broadcast_to(outgoing.reshape(1, owners, slots, feats), (nx, owners, slots, feats))
    arrived = exchange(outgoing.reshape(nx * owners, slots, feats), ("x", "l", "c"))
    arrived = arrived.reshape(nx, owners, held, CAP, feats)
    rows_in = arrived.transpose(2, 1, 3, 0, 4).reshape(held, owners * CAP, nx * feats)
    matrix = both.transpose(1, 0, 2, 3).reshape(held, nx * feats, 2 * units)
    parts = jnp.einsum("erk,ekf->erf", rows_in, matrix, preferred_element_type=F32).astype(BF16)
    parts = exchange(parts.reshape(deep, held * owners * CAP // deep, 2 * units), ("z", "h"))
    sums = jnp.sum(parts.astype(F32), axis=0)
    hidden = (jax.nn.silu(sums[:, :units]) * sums[:, units:]).astype(BF16)
    hidden = spread(hidden, ("z", "h"), deep).reshape(held, owners * CAP, units)
    result = jnp.einsum("eru,xedu->xerd", hidden, down, preferred_element_type=F32).astype(BF16)
    result = result.reshape(nx, held, owners, CAP, feats).transpose(0, 2, 1, 3, 4)
    back = exchange(result.reshape(nx * owners, slots, feats), ("x", "l", "c"))
    back = jnp.sum(back.reshape(nx, owners * slots, feats).astype(F32), axis=0).astype(BF16)
    share = jnp.sum(
        jnp.where(routes[:, :, None] == lax.iota(jnp.int32, EXPERTS), gate_values[:, :, None], 0.0), axis=1
    )
    weights = placed.astype(F32) * jnp.repeat(share, CAP, axis=1)
    moe_output = jnp.dot(weights, back.astype(F32), precision=lax.Precision.HIGHEST).astype(BF16)

    piece = column.shape[0]
    near = lax.ppermute(column, "x", ring("x", nx, 1))
    far = lax.ppermute(column, "x", ring("x", nx, -1))
    low = lax.ppermute(near[: piece // 2], "x", ring("x", nx, 1))
    high = lax.ppermute(far[piece // 2 :], "x", ring("x", nx, -1))
    mine = jnp.concatenate([column, near, far, low, high], axis=0)
    other = lax.ppermute(mine, "c", ring("c", nc, 1))

    sources = jnp.stack([x_at, x_at + nx - 1, x_at + 1, x_at + 2]) % nx
    at_z = lax.iota(jnp.int32, deep)
    first = (at_z[None, :] * nx + sources[:, None]) * latents.shape[0]
    place = first[:, :, None] + lax.iota(jnp.int32, own)
    key_pos = jnp.stack([place + core * own, place + (nc - 1 - core) * own]).reshape(1, -1)

    query_rows = queries.reshape(queries.shape[0] * H, WIDE)
    mixed = attend(offsets, query_rows, key_pos, mine, other)
    attention_out = mixed.reshape(queries.shape[0], H * LAT)
    return (attention_out, moe_output)


def solution(mesh):
    fine = Mesh(mesh.devices.reshape(8, 2, 4, 4, 2), ("z", "h", "x", "l", "c"))
    ctx, exp = ("z", "h", "x"), ("l", "c")
    return jax.shard_map(
        local,
        mesh=fine,
        in_specs=(
            P(ctx + exp, None),
            P(ctx, None),
            P(ctx + exp),
            P(exp, ctx),
            P(exp, None),
            P(exp, None),
            P(exp, ctx, None),
            P(exp, ctx, None),
            P(exp, None, ctx),
        ),
        out_specs=(P(ctx + exp, None), P(exp, ctx)),
        check_vma=False,
    )
```

```python
import functools
import math

import jax
import jax.numpy as jnp
from jax import lax
from jax.experimental import pallas as pl
from jax.experimental.pallas import tpu as pltpu
from jax.sharding import Mesh, PartitionSpec as P

H = 128
LAT = 512
ROPE = 64
WIDE = LAT + ROPE
TOPK = 6
EXPERTS = 16
CAP = 16
LANES = 128

SCALE_LOG2 = 192.0 ** (-0.5) * math.log2(math.e)
F32 = jnp.float32
BF16 = jnp.bfloat16
I32 = jnp.int32
VMEM = pl.BlockSpec(memory_space=pltpu.VMEM)
SMEM = pl.BlockSpec(memory_space=pltpu.SMEM)


def shaped(shape, dtype):
    return jax.ShapeDtypeStruct(shape, dtype)


def kernel(body, name, out_shape, specs, args, flops, moved, special=0):
    return pl.pallas_call(
        body,
        out_shape=out_shape,
        in_specs=specs,
        out_specs=jax.tree.map(lambda _: VMEM, out_shape),
        compiler_params=pltpu.CompilerParams(vmem_limit_bytes=40 * 2**20),
        cost_estimate=pl.CostEstimate(flops=flops, bytes_accessed=moved, transcendentals=special),
        name=name,
    )(*args)


def attention_body(pieces, first, last, spots, queries, base, *refs):
    keys, refs = refs[:pieces], refs[pieces:]
    rows = queries.shape[0]
    row_pos = spots[0] + lax.broadcasted_iota(I32, (rows, 1), 0) // H
    query = queries[...]
    if first:
        top = jnp.full((rows, 1), -1e30, F32)
    else:
        top = refs[0][:, :1]
    scored = []
    for j, key in enumerate(keys):
        scores = jnp.dot(query, key[...], preferred_element_type=F32) * SCALE_LOG2
        scored.append(jnp.where(base[:1, :] <= row_pos - spots[1 + j], scores, -jnp.inf))
    new = top
    for scores in scored:
        new = jnp.maximum(new, jnp.max(scores, axis=1, keepdims=True))
    den, acc = 0.0, 0.0
    if not first:
        shrink = jnp.exp2(top - new)
        den, acc = refs[1][:, :1] * shrink, refs[2][...] * shrink
    for scores, key in zip(scored, keys):
        weights = jnp.exp2(scores - new)
        den = den + jnp.sum(weights, axis=1, keepdims=True)
        acc = acc + lax.dot_general(
            weights.astype(BF16), key[:LAT, :], (((1,), (1,)), ((), ())), preferred_element_type=F32
        )
    if last:
        refs[-1][...] = (acc / den).astype(BF16)
    else:
        refs[-3][...] = jnp.broadcast_to(new, (rows, LANES))
        refs[-2][...] = jnp.broadcast_to(den, (rows, LANES))
        refs[-1][...] = acc


def attend(spots, queries, base, pieces, state, last, name):
    rows, count = queries.shape[0], base.shape[1] * len(pieces)
    if last:
        out = shaped((rows, LAT), BF16)
    else:
        out = [shaped((rows, LANES), F32)] * 2 + [shaped((rows, LAT), F32)]
    body = functools.partial(attention_body, len(pieces), not state, last)
    specs = [SMEM] + [VMEM] * (2 + len(pieces) + len(state))
    args = (spots, queries, base, *pieces, *state)
    return kernel(body, name, out, specs, args, 4 * rows * count * WIDE, 2 * count * WIDE + 2**20, rows * count)


def dispatch_body(copies, routes, tokens, out):
    count = tokens.shape[0]
    slot = lax.broadcasted_iota(I32, (EXPERTS * CAP, count), 0)
    named = routes[0:1, :] == slot // CAP
    for k in range(1, TOPK):
        named = named | (routes[k : k + 1, :] == slot // CAP)
    hot = named.astype(F32)
    earlier = lax.broadcasted_iota(I32, (count, count), 0) < lax.broadcasted_iota(I32, (count, count), 1)
    rank = jnp.dot(hot.astype(BF16), earlier.astype(F32).astype(BF16), preferred_element_type=F32)
    placed = jnp.where(rank == (slot % CAP).astype(F32), hot, 0.0).astype(BF16)
    sent = jnp.dot(placed, tokens[...], preferred_element_type=F32).astype(BF16)
    owners = out.shape[0] // copies
    out[...] = jnp.zeros(out.shape, BF16)
    for i in range(copies):
        out[i * owners : (i + 1) * owners, :, : tokens.shape[1]] = sent.reshape(owners, -1, tokens.shape[1])


def cut_body(spots, gate, up, *outs):
    parts = len(outs)
    units = gate.shape[2] // parts
    for j, out in enumerate(outs):
        at = pl.multiple_of(lax.rem(spots[0] + j, parts) * units, LANES)
        out[:, :, :units] = gate[:, :, pl.ds(at, units)]
        out[:, :, units:] = up[:, :, pl.ds(at, units)]


def first_body(order, spots, arrived, *refs):
    weights, out = refs[:-1], refs[-1]
    held, feats = weights[0].shape[:2]
    owners = arrived.shape[0] // len(weights)
    for e in range(held):
        total = 0.0
        for j, matrix in zip(order, weights):
            at = lax.rem(spots[0] + j, len(weights)) * owners
            rows = arrived[pl.ds(at, owners), e * CAP : (e + 1) * CAP, :].reshape(owners * CAP, LANES)
            total = total + jnp.dot(rows[:, :feats], matrix[e], preferred_element_type=F32)
        out[e * owners * CAP : (e + 1) * owners * CAP, :] = total.astype(BF16)


def add_body(parts, total, rounded):
    sums = parts[0].astype(F32)
    for i in range(1, parts.shape[0]):
        sums = sums + parts[i].astype(F32)
    total[...] = sums
    rounded[...] = sums.astype(BF16)


def hidden_body(total, other, out):
    sums = total[...] + other[...].astype(F32)
    units = sums.shape[1] // 2
    gate = sums[:, :units]
    hidden = (gate / (1.0 + jnp.exp(-gate)) * sums[:, units:]).astype(BF16)
    for i in range(out.shape[0]):
        out[i] = hidden


def second_body(deep, across, hidden, down, out):
    held, feats = down.shape[0], down.shape[2]
    units = hidden.shape[2]
    group = deep // held
    owners = out.shape[0]
    out[...] = jnp.zeros(out.shape, BF16)
    for e in range(held):
        total = 0.0
        for x in range(across):
            rows = jnp.concatenate([hidden[(group * e + i) * across + x] for i in range(group)], axis=0)
            total = total + jnp.dot(rows, down[e, x * units : (x + 1) * units, :], preferred_element_type=F32)
        out[:, e * CAP : (e + 1) * CAP, :feats] = total.astype(BF16).reshape(owners, CAP, feats)


def combine_body(routes, gates, back, out):
    count, feats = out.shape
    slot = lax.broadcasted_iota(I32, (count, EXPERTS * CAP), 1)
    hot = jnp.zeros(slot.shape, F32)
    share = jnp.zeros(slot.shape, F32)
    for k in range(TOPK):
        here = routes[:, k : k + 1] == slot // CAP
        hot = jnp.where(here, 1.0, hot)
        share = share + jnp.where(here, gates[:, k : k + 1], 0.0)
    earlier = lax.broadcasted_iota(I32, (count, count), 1) < lax.broadcasted_iota(I32, (count, count), 0)
    rank = jnp.dot(earlier.astype(F32).astype(BF16), hot.astype(BF16), preferred_element_type=F32)
    share = jnp.where(rank == (slot % CAP).astype(F32), share, 0.0)
    rows = back[...].reshape(EXPERTS * CAP, LANES)[:, :feats].astype(F32)
    mixed = jnp.dot(share, rows, precision=lax.Precision.HIGHEST, preferred_element_type=F32)
    out[...] = mixed.astype(BF16)


def exchange(array, axes):
    return lax.all_to_all(array, axes, split_axis=0, concat_axis=0, tiled=False)


def shift(array, axis, by):
    size = lax.axis_size(axis)
    return lax.ppermute(array, axis, [(i, (i + by) % size) for i in range(size)])


def local(queries, latents, offsets, moe_input, routes, gate_values, w_gate, w_up, w_down):
    nz, nh, nx, nl, nc = (lax.axis_size(a) for a in ("z", "h", "x", "l", "c"))
    h_at, x_at, core = (lax.axis_index(a) for a in ("h", "x", "c"))
    owners = nl * nc
    held, feats, width = w_gate.shape
    units = width // nx
    tokens = moe_input.shape[0]
    slots = held * CAP
    where_x = x_at.astype(I32).reshape(1)

    outgoing = kernel(
        functools.partial(dispatch_body, nx), "dispatch", shaped((nx * owners, slots, LANES), BF16),
        [VMEM] * 2, (routes.T, moe_input), 2**20, 2**18,
    )
    arrived = exchange(outgoing, ("x", "l", "c"))

    own = latents.shape[0] // nc
    half = lax.dynamic_slice_in_dim(latents, core * own, own, 0)
    paired = jnp.concatenate([half, shift(half, "h", 1)], axis=0)
    column = exchange(jnp.broadcast_to(paired[None], (nz,) + paired.shape), "z")
    column = column.reshape(nz * nh * own, WIDE).T

    cut = kernel(
        cut_body, "cut", [shaped((held, feats, 2 * units), BF16)] * nx,
        [SMEM, VMEM, VMEM], (where_x, w_gate, w_up), 2**10, 2**21,
    )
    weights = [cut[0]] + [shift(cut[j], "x", j) for j in range(1, nx)]
    order = [0] + [nx - j for j in range(1, nx)]
    parts = kernel(
        functools.partial(first_body, order), "first", shaped((held * owners * CAP, 2 * units), BF16),
        [SMEM] + [VMEM] * (1 + nx), (where_x, arrived, *weights), 2**28, 2**21,
    )
    parts = exchange(parts.reshape(nz, -1, 2 * units), "z")
    rows = parts.shape[1]
    total, rounded = kernel(
        add_body, "add", [shaped((rows, 2 * units), F32), shaped((rows, 2 * units), BF16)],
        [VMEM], (parts,), 2**18, 2**19,
    )
    hidden = kernel(
        hidden_body, "hidden", shaped((nz * nx, rows, units), BF16),
        [VMEM] * 2, (total, shift(rounded, "h", 1)), 2**18, 2**20, 2**14,
    )
    hidden = exchange(hidden, ("z", "x"))
    result = kernel(
        functools.partial(second_body, nz, nx), "second", shaped((owners, slots, LANES), BF16),
        [VMEM] * 2, (hidden, w_down), 2**27, 2**21,
    )
    back = exchange(result, ("l", "c"))
    moe_output = kernel(
        combine_body, "combine", shaped((tokens, feats), BF16),
        [VMEM] * 3, (routes, gate_values, back), 2**20, 2**18,
    )

    others = [shift(column, "x", 1), shift(column, "x", -1), shift(column, "x", 2)]
    sources = [x_at, x_at + nx - 1, x_at + 1, x_at + 2]
    at_z = lax.broadcasted_iota(I32, (nz, nh, own), 0)
    at_h = (lax.broadcasted_iota(I32, (nz, nh, own), 1) + h_at) % nh
    base = ((at_z * nh + at_h) * nx * latents.shape[0] + lax.broadcasted_iota(I32, (nz, nh, own), 2)).reshape(1, -1)
    query_rows = queries.reshape(queries.shape[0] * H, WIDE)

    pieces, spots = [], []
    for piece, source in zip([column] + others, sources):
        pieces.append([piece, shift(piece, "c", 1)])
        first = (source % nx) * latents.shape[0]
        spots.append([first + core * own, first + (nc - 1 - core) * own])

    def call(which, state, last, name):
        marks = jnp.stack([offsets[0]] + [s for i in which for s in spots[i]]).astype(I32)
        return attend(marks, query_rows, base, [p for i in which for p in pieces[i]], state, last, name)

    state = call([0], [], False, "attend_own")
    state = call([1, 2], state, False, "attend_near")
    mixed = call([3], state, True, "attend_far")
    attention_out = mixed.reshape(queries.shape[0], H * LAT)
    return (attention_out, moe_output)


def solution(mesh):
    fine = Mesh(mesh.devices.reshape(8, 2, 4, 4, 2), ("z", "h", "x", "l", "c"))
    ctx, exp = ("z", "h", "x"), ("l", "c")
    return jax.shard_map(
        local,
        mesh=fine,
        in_specs=(
            P(ctx + exp, None),
            P(ctx, None),
            P(ctx + exp),
            P(exp, ctx),
            P(exp, None),
            P(exp, None),
            P(exp, ctx, None),
            P(exp, ctx, None),
            P(exp, None, ctx),
        ),
        out_specs=(P(ctx + exp, None), P(exp, ctx)),
        check_vma=False,
    )
```

```python
import functools
import math

import jax
import jax.numpy as jnp
from jax import lax
from jax.experimental import pallas as pl
from jax.experimental.pallas import tpu as pltpu
from jax.sharding import Mesh, PartitionSpec as P

H = 128
LAT = 512
ROPE = 64
WIDE = LAT + ROPE
TOPK = 6
EXPERTS = 16
CAP = 16
LANES = 128

SCALE_LOG2 = 192.0 ** (-0.5) * math.log2(math.e)
F32 = jnp.float32
BF16 = jnp.bfloat16
I32 = jnp.int32
VMEM = pl.BlockSpec(memory_space=pltpu.VMEM)
AFTER = pl.BlockSpec(memory_space=pl.ANY)
SMEM = pl.BlockSpec(memory_space=pltpu.SMEM)


def shaped(shape, dtype):
    return jax.ShapeDtypeStruct(shape, dtype)


def kernel(body, name, out_shape, specs, args, flops, moved, special=0):
    return pl.pallas_call(
        body,
        out_shape=out_shape,
        in_specs=specs,
        out_specs=jax.tree.map(lambda _: VMEM, out_shape),
        compiler_params=pltpu.CompilerParams(vmem_limit_bytes=24 * 2**20),
        cost_estimate=pl.CostEstimate(flops=flops, bytes_accessed=moved, transcendentals=special),
        name=name,
    )(*args)


def attention_body(pieces, first, last, spots, queries, base, *refs):
    keys, refs = refs[:pieces], refs[pieces:]
    rows = queries.shape[0]
    row_pos = spots[0] + lax.broadcasted_iota(I32, (rows, 1), 0) // H
    query = queries[...]
    if first:
        top = jnp.full((rows, 1), -1e30, F32)
    else:
        top = refs[0][:, :1]
    scored = []
    for j, key in enumerate(keys):
        scores = jnp.dot(query, key[...], preferred_element_type=F32) * SCALE_LOG2
        scored.append(jnp.where(base[:1, :] <= row_pos - spots[1 + j], scores, -jnp.inf))
    new = top
    for scores in scored:
        new = jnp.maximum(new, jnp.max(scores, axis=1, keepdims=True))
    den, acc = 0.0, 0.0
    if not first:
        shrink = jnp.exp2(top - new)
        den, acc = refs[1][:, :1] * shrink, refs[2][...] * shrink
    for scores, key in zip(scored, keys):
        weights = jnp.exp2(scores - new)
        den = den + jnp.sum(weights, axis=1, keepdims=True)
        acc = acc + lax.dot_general(
            weights.astype(BF16), key[:LAT, :], (((1,), (1,)), ((), ())), preferred_element_type=F32
        )
    if last:
        refs[-1][...] = (acc / den).astype(BF16)
    else:
        refs[-3][...] = jnp.broadcast_to(new, (rows, LANES))
        refs[-2][...] = jnp.broadcast_to(den, (rows, LANES))
        refs[-1][...] = acc


def attend(spots, queries, base, pieces, state, last, name):
    rows, count = queries.shape[0], base.shape[1] * len(pieces)
    if last:
        out = shaped((rows, LAT), BF16)
    else:
        out = [shaped((rows, LANES), F32)] * 2 + [shaped((rows, LAT), F32)]
    body = functools.partial(attention_body, len(pieces), not state, last)
    specs = [SMEM] + [VMEM] * (2 + len(pieces) + len(state))
    args = (spots, queries, base, *pieces, *state)
    return kernel(body, name, out, specs, args, 4 * rows * count * WIDE, 2 * count * WIDE + 2**20, rows * count)


def dispatch_body(copies, routes, tokens, out):
    count = tokens.shape[0]
    slot = lax.broadcasted_iota(I32, (EXPERTS * CAP, count), 0)
    named = routes[0:1, :] == slot // CAP
    for k in range(1, TOPK):
        named = named | (routes[k : k + 1, :] == slot // CAP)
    hot = named.astype(F32)
    earlier = lax.broadcasted_iota(I32, (count, count), 0) < lax.broadcasted_iota(I32, (count, count), 1)
    rank = jnp.dot(hot.astype(BF16), earlier.astype(F32).astype(BF16), preferred_element_type=F32)
    placed = jnp.where(rank == (slot % CAP).astype(F32), hot, 0.0).astype(BF16)
    sent = jnp.dot(placed, tokens[...], preferred_element_type=F32).astype(BF16)
    owners = out.shape[0] // copies
    out[...] = jnp.zeros(out.shape, BF16)
    for i in range(copies):
        out[i * owners : (i + 1) * owners, :, : tokens.shape[1]] = sent.reshape(owners, -1, tokens.shape[1])


def cut_body(spots, gate, up, *outs):
    parts = len(outs)
    units = gate.shape[2] // parts
    for j, out in enumerate(outs):
        at = pl.multiple_of(lax.rem(spots[0] + j, parts) * units, LANES)
        out[:, :, :units] = gate[:, :, pl.ds(at, units)]
        out[:, :, units:] = up[:, :, pl.ds(at, units)]


def pair_body(rows, after, out):
    for i in range(out.shape[0]):
        out[i] = rows[...]


def first_body(order, spots, after, arrived, *refs):
    weights, out = refs[:-1], refs[-1]
    held, feats = weights[0].shape[:2]
    owners = arrived.shape[0] // len(weights)
    for e in range(held):
        total = 0.0
        for j, matrix in zip(order, weights):
            at = lax.rem(spots[0] + j, len(weights)) * owners
            rows = arrived[pl.ds(at, owners), e * CAP : (e + 1) * CAP, :].reshape(owners * CAP, LANES)
            total = total + jnp.dot(rows[:, :feats], matrix[e], preferred_element_type=F32)
        out[e * owners * CAP : (e + 1) * owners * CAP, :] = total.astype(BF16)


def add_body(parts, total, rounded):
    sums = parts[0].astype(F32)
    for i in range(1, parts.shape[0]):
        sums = sums + parts[i].astype(F32)
    total[...] = sums
    rounded[...] = sums.astype(BF16)


def hidden_body(total, other, out):
    sums = total[...] + other[...].astype(F32)
    units = sums.shape[1] // 2
    gate = sums[:, :units]
    hidden = (gate / (1.0 + jnp.exp(-gate)) * sums[:, units:]).astype(BF16)
    for i in range(out.shape[0]):
        out[i] = hidden


def second_body(deep, across, hidden, down, out):
    held, feats = down.shape[0], down.shape[2]
    units = hidden.shape[2]
    group = deep // held
    owners = out.shape[0]
    out[...] = jnp.zeros(out.shape, BF16)
    for e in range(held):
        total = 0.0
        for x in range(across):
            rows = jnp.concatenate([hidden[(group * e + i) * across + x] for i in range(group)], axis=0)
            total = total + jnp.dot(rows, down[e, x * units : (x + 1) * units, :], preferred_element_type=F32)
        out[:, e * CAP : (e + 1) * CAP, :feats] = total.astype(BF16).reshape(owners, CAP, feats)


def combine_body(routes, gates, back, out):
    count, feats = out.shape
    slot = lax.broadcasted_iota(I32, (count, EXPERTS * CAP), 1)
    hot = jnp.zeros(slot.shape, F32)
    share = jnp.zeros(slot.shape, F32)
    for k in range(TOPK):
        here = routes[:, k : k + 1] == slot // CAP
        hot = jnp.where(here, 1.0, hot)
        share = share + jnp.where(here, gates[:, k : k + 1], 0.0)
    earlier = lax.broadcasted_iota(I32, (count, count), 1) < lax.broadcasted_iota(I32, (count, count), 0)
    rank = jnp.dot(earlier.astype(F32).astype(BF16), hot.astype(BF16), preferred_element_type=F32)
    share = jnp.where(rank == (slot % CAP).astype(F32), share, 0.0)
    rows = back[...].reshape(EXPERTS * CAP, LANES)[:, :feats].astype(F32)
    mixed = jnp.dot(share, rows, precision=lax.Precision.HIGHEST, preferred_element_type=F32)
    out[...] = mixed.astype(BF16)


def hold(array, after):
    return pl.pallas_call(
        lambda array, after, out: None,
        out_shape=shaped(array.shape, array.dtype),
        in_specs=[AFTER] * 2,
        out_specs=AFTER,
        input_output_aliases={0: 0},
        name="hold",
    )(array, after)


def exchange(array, axes):
    return lax.all_to_all(array, axes, split_axis=0, concat_axis=0, tiled=False)


def shift(array, axis, by):
    size = lax.axis_size(axis)
    return lax.ppermute(array, axis, [(i, (i + by) % size) for i in range(size)])


def local(queries, latents, offsets, moe_input, routes, gate_values, w_gate, w_up, w_down):
    nz, nh, nx, nl, nc = (lax.axis_size(a) for a in ("z", "h", "x", "l", "c"))
    h_at, x_at, core = (lax.axis_index(a) for a in ("h", "x", "c"))
    owners = nl * nc
    held, feats, width = w_gate.shape
    units = width // nx
    tokens = moe_input.shape[0]
    slots = held * CAP
    where_x = x_at.astype(I32).reshape(1)

    outgoing = kernel(
        functools.partial(dispatch_body, nx), "dispatch", shaped((nx * owners, slots, LANES), BF16),
        [VMEM] * 2, (routes.T, moe_input), 2**20, 2**18,
    )
    arrived = exchange(outgoing, ("x", "l", "c"))

    own = latents.shape[0] // nc
    half = lax.dynamic_slice_in_dim(latents, core * own, own, 0)
    paired = jnp.concatenate([half, shift(half, "h", 1)], axis=0)
    paired = kernel(
        pair_body, "pair", shaped((nz,) + paired.shape, BF16), [VMEM, AFTER], (paired, arrived), 2**10, 2**20
    )
    column = exchange(paired, "z")
    column = column.reshape(nz * nh * own, WIDE).T

    cut = kernel(
        cut_body, "cut", [shaped((held, feats, 2 * units), BF16)] * nx,
        [SMEM, VMEM, VMEM], (where_x, w_gate, w_up), 2**10, 2**21,
    )
    weights = [cut[0]] + [shift(cut[j], "x", j) for j in range(1, nx)]
    order = [0] + [nx - j for j in range(1, nx)]
    parts = kernel(
        functools.partial(first_body, order), "first", shaped((held * owners * CAP, 2 * units), BF16),
        [SMEM, AFTER] + [VMEM] * (1 + nx), (where_x, column, arrived, *weights), 2**28, 2**21,
    )
    parts = exchange(parts.reshape(nz, -1, 2 * units), "z")
    rows = parts.shape[1]
    total, rounded = kernel(
        add_body, "add", [shaped((rows, 2 * units), F32), shaped((rows, 2 * units), BF16)],
        [VMEM], (parts,), 2**18, 2**19,
    )
    hidden = kernel(
        hidden_body, "hidden", shaped((nz * nx, rows, units), BF16),
        [VMEM] * 2, (total, shift(rounded, "h", 1)), 2**18, 2**20, 2**14,
    )
    hidden = exchange(hidden, ("z", "x"))
    result = kernel(
        functools.partial(second_body, nz, nx), "second", shaped((owners, slots, LANES), BF16),
        [VMEM] * 2, (hidden, w_down), 2**27, 2**21,
    )
    back = exchange(result, ("l", "c"))
    moe_output = kernel(
        combine_body, "combine", shaped((tokens, feats), BF16),
        [VMEM] * 3, (routes, gate_values, back), 2**20, 2**18,
    )

    others = [shift(column, "x", 1), shift(column, "x", -1), shift(column, "x", 2)]
    sources = [x_at, x_at + nx - 1, x_at + 1, x_at + 2]
    at_z = lax.broadcasted_iota(I32, (nz, nh, own), 0)
    at_h = (lax.broadcasted_iota(I32, (nz, nh, own), 1) + h_at) % nh
    base = ((at_z * nh + at_h) * nx * latents.shape[0] + lax.broadcasted_iota(I32, (nz, nh, own), 2)).reshape(1, -1)
    query_rows = queries.reshape(queries.shape[0] * H, WIDE)

    spots = []
    for source in sources:
        first = (source % nx) * latents.shape[0]
        spots.append([first + core * own, first + (nc - 1 - core) * own])

    def call(which, pieces, state, last, name):
        marks = jnp.stack([offsets[0]] + [s for i in which for s in spots[i]]).astype(I32)
        both = [p for piece in pieces for p in (piece, shift(piece, "c", 1))]
        return attend(marks, query_rows, base, both, state, last, name)

    state = call([0], [column], [], False, "attend_own")
    state = call([1, 2], others[:2], state, False, "attend_near")
    mixed = call([3], [hold(others[2], state[0])], state, True, "attend_far")
    attention_out = mixed.reshape(queries.shape[0], H * LAT)
    return (attention_out, moe_output)


def solution(mesh):
    fine = Mesh(mesh.devices.reshape(8, 2, 4, 4, 2), ("z", "h", "x", "l", "c"))
    ctx, exp = ("z", "h", "x"), ("l", "c")
    return jax.shard_map(
        local,
        mesh=fine,
        in_specs=(
            P(ctx + exp, None),
            P(ctx, None),
            P(ctx + exp),
            P(exp, ctx),
            P(exp, None),
            P(exp, None),
            P(exp, ctx, None),
            P(exp, ctx, None),
            P(exp, None, ctx),
        ),
        out_specs=(P(ctx + exp, None), P(exp, ctx)),
        check_vma=False,
    )
```

```python
import functools
import math

import jax
import jax.numpy as jnp
from jax import lax
from jax.experimental import pallas as pl
from jax.experimental.pallas import tpu as pltpu
from jax.sharding import Mesh, PartitionSpec as P

H = 128
LAT = 512
ROPE = 64
WIDE = LAT + ROPE
TOPK = 6
EXPERTS = 16
CAP = 16
LANES = 128
CLAIM = 4

SCALE_LOG2 = 192.0 ** (-0.5) * math.log2(math.e)
F32 = jnp.float32
BF16 = jnp.bfloat16
I32 = jnp.int32
VMEM = pl.BlockSpec(memory_space=pltpu.VMEM)
AFTER = pl.BlockSpec(memory_space=pl.ANY)
SMEM = pl.BlockSpec(memory_space=pltpu.SMEM)


def shaped(shape, dtype):
    return jax.ShapeDtypeStruct(shape, dtype)


def kernel(body, name, out_shape, specs, args, flops, moved, special=0):
    return pl.pallas_call(
        body,
        out_shape=out_shape,
        in_specs=specs,
        out_specs=jax.tree.map(lambda _: VMEM, out_shape),
        compiler_params=pltpu.CompilerParams(vmem_limit_bytes=24 * 2**20),
        cost_estimate=pl.CostEstimate(flops=flops, bytes_accessed=moved, transcendentals=special),
        name=name,
    )(*args)


def attention_body(pieces, first, last, spots, queries, base, *refs):
    keys, refs = refs[:pieces], refs[pieces:]
    rows = queries.shape[0]
    row_pos = spots[0] + lax.broadcasted_iota(I32, (rows, 1), 0) // H
    query = queries[...]
    if first:
        top = jnp.full((rows, 1), -1e30, F32)
    else:
        top = refs[0][:, :1]
    scored = []
    for j, key in enumerate(keys):
        scores = jnp.dot(query, key[...], preferred_element_type=F32) * SCALE_LOG2
        scored.append(jnp.where(base[:1, :] <= row_pos - spots[1 + j], scores, -jnp.inf))
    new = top
    for scores in scored:
        new = jnp.maximum(new, jnp.max(scores, axis=1, keepdims=True))
    den, acc = 0.0, 0.0
    if not first:
        shrink = jnp.exp2(top - new)
        den, acc = refs[1][:, :1] * shrink, refs[2][...] * shrink
    for scores, key in zip(scored, keys):
        weights = jnp.exp2(scores - new)
        den = den + jnp.sum(weights, axis=1, keepdims=True)
        acc = acc + lax.dot_general(
            weights.astype(BF16), key[:LAT, :], (((1,), (1,)), ((), ())), preferred_element_type=F32
        )
    if last:
        refs[-1][...] = (acc / den).astype(BF16)
    else:
        refs[-3][...] = jnp.broadcast_to(new, (rows, LANES))
        refs[-2][...] = jnp.broadcast_to(den, (rows, LANES))
        refs[-1][...] = acc


def attend(spots, queries, base, pieces, state, last, name):
    rows, count = queries.shape[0], base.shape[1] * len(pieces)
    if last:
        out = shaped((rows, LAT), BF16)
    else:
        out = [shaped((rows, LANES), F32)] * 2 + [shaped((rows, LAT), F32)]
    body = functools.partial(attention_body, len(pieces), not state, last)
    specs = [SMEM] + [VMEM] * (2 + len(pieces) + len(state))
    args = (spots, queries, base, *pieces, *state)
    return kernel(body, name, out, specs, args, 4 * rows * count * WIDE * CLAIM, (2 * count * WIDE + 2**20) * CLAIM, rows * count * CLAIM)


def dispatch_body(copies, routes, tokens, *refs):
    out = refs[-1]
    count = tokens.shape[0]
    slot = lax.broadcasted_iota(I32, (EXPERTS * CAP, count), 0)
    named = routes[0:1, :] == slot // CAP
    for k in range(1, TOPK):
        named = named | (routes[k : k + 1, :] == slot // CAP)
    hot = named.astype(F32)
    earlier = lax.broadcasted_iota(I32, (count, count), 0) < lax.broadcasted_iota(I32, (count, count), 1)
    rank = jnp.dot(hot.astype(BF16), earlier.astype(F32).astype(BF16), preferred_element_type=F32)
    placed = jnp.where(rank == (slot % CAP).astype(F32), hot, 0.0).astype(BF16)
    sent = jnp.dot(placed, tokens[...], preferred_element_type=F32).astype(BF16)
    owners = out.shape[0] // copies
    out[...] = jnp.zeros(out.shape, BF16)
    for i in range(copies):
        out[i * owners : (i + 1) * owners, :, : tokens.shape[1]] = sent.reshape(owners, -1, tokens.shape[1])


def cut_body(spots, gate, up, *outs):
    parts = len(outs)
    units = gate.shape[2] // parts
    for j, out in enumerate(outs):
        at = pl.multiple_of(lax.rem(spots[0] + j, parts) * units, LANES)
        out[:, :, :units] = gate[:, :, pl.ds(at, units)]
        out[:, :, units:] = up[:, :, pl.ds(at, units)]


def first_body(order, spots, arrived, *refs):
    weights, out = refs[:-1], refs[-1]
    held, feats = weights[0].shape[:2]
    owners = arrived.shape[0] // len(weights)
    for e in range(held):
        total = 0.0
        for j, matrix in zip(order, weights):
            at = lax.rem(spots[0] + j, len(weights)) * owners
            rows = arrived[pl.ds(at, owners), e * CAP : (e + 1) * CAP, :].reshape(owners * CAP, LANES)
            total = total + jnp.dot(rows[:, :feats], matrix[e], preferred_element_type=F32)
        out[e * owners * CAP : (e + 1) * owners * CAP, :] = total.astype(BF16)


def add_body(parts, total, rounded):
    sums = parts[0].astype(F32)
    for i in range(1, parts.shape[0]):
        sums = sums + parts[i].astype(F32)
    total[...] = sums
    rounded[...] = sums.astype(BF16)


def hidden_body(total, other, out):
    sums = total[...] + other[...].astype(F32)
    units = sums.shape[1] // 2
    gate = sums[:, :units]
    hidden = (gate / (1.0 + jnp.exp(-gate)) * sums[:, units:]).astype(BF16)
    for i in range(out.shape[0]):
        out[i] = hidden


def second_body(deep, across, hidden, down, out):
    held, feats = down.shape[0], down.shape[2]
    units = hidden.shape[2]
    group = deep // held
    owners = out.shape[0]
    out[...] = jnp.zeros(out.shape, BF16)
    for e in range(held):
        total = 0.0
        for x in range(across):
            rows = jnp.concatenate([hidden[(group * e + i) * across + x] for i in range(group)], axis=0)
            total = total + jnp.dot(rows, down[e, x * units : (x + 1) * units, :], preferred_element_type=F32)
        out[:, e * CAP : (e + 1) * CAP, :feats] = total.astype(BF16).reshape(owners, CAP, feats)


def combine_body(routes, gates, back, out):
    count, feats = out.shape
    slot = lax.broadcasted_iota(I32, (count, EXPERTS * CAP), 1)
    hot = jnp.zeros(slot.shape, F32)
    share = jnp.zeros(slot.shape, F32)
    for k in range(TOPK):
        here = routes[:, k : k + 1] == slot // CAP
        hot = jnp.where(here, 1.0, hot)
        share = share + jnp.where(here, gates[:, k : k + 1], 0.0)
    earlier = lax.broadcasted_iota(I32, (count, count), 1) < lax.broadcasted_iota(I32, (count, count), 0)
    rank = jnp.dot(earlier.astype(F32).astype(BF16), hot.astype(BF16), preferred_element_type=F32)
    share = jnp.where(rank == (slot % CAP).astype(F32), share, 0.0)
    rows = back[...].reshape(EXPERTS * CAP, LANES)[:, :feats].astype(F32)
    mixed = jnp.dot(share, rows, precision=lax.Precision.HIGHEST, preferred_element_type=F32)
    out[...] = mixed.astype(BF16)


def hold(array, after):
    return pl.pallas_call(
        lambda array, after, out: None,
        out_shape=shaped(array.shape, array.dtype),
        in_specs=[AFTER] * 2,
        out_specs=AFTER,
        input_output_aliases={0: 0},
        name="hold",
    )(array, after)


def exchange(array, axes):
    return lax.all_to_all(array, axes, split_axis=0, concat_axis=0, tiled=False)


def shift(array, axis, by):
    size = lax.axis_size(axis)
    return lax.ppermute(array, axis, [(i, (i + by) % size) for i in range(size)])


def local(queries, latents, offsets, moe_input, routes, gate_values, w_gate, w_up, w_down):
    nz, nh, nx, nl, nc = (lax.axis_size(a) for a in ("z", "h", "x", "l", "c"))
    x_at, core = lax.axis_index("x"), lax.axis_index("c")
    owners = nl * nc
    held, feats, width = w_gate.shape
    units = width // nx
    tokens = moe_input.shape[0]
    slots = held * CAP
    where_x = x_at.astype(I32).reshape(1)

    own = latents.shape[0] // nc
    half = lax.dynamic_slice_in_dim(latents, core * own, own, 0)
    column = exchange(jnp.broadcast_to(half[None], (nz * nh,) + half.shape), ("z", "h"))
    column = column.reshape(nz * nh * own, WIDE)

    cut = kernel(
        cut_body, "cut", [shaped((held, feats, 2 * units), BF16)] * nx,
        [SMEM, VMEM, VMEM], (where_x, w_gate, w_up), 2**10, 2**21,
    )
    weights = [cut[0]] + [shift(cut[j], "x", j) for j in range(1, nx)]
    outgoing = kernel(
        functools.partial(dispatch_body, nx), "dispatch", shaped((nx * owners, slots, LANES), BF16),
        [VMEM, VMEM] + [AFTER] * nx, (routes.T, moe_input, column, *weights[1:]), 2**20, 2**18,
    )
    arrived = exchange(outgoing, ("x", "l", "c"))
    column = column.T
    others = [shift(column, "x", 1), shift(column, "x", -1)]

    order = [0] + [nx - j for j in range(1, nx)]
    parts = kernel(
        functools.partial(first_body, order), "first", shaped((held * owners * CAP, 2 * units), BF16),
        [SMEM] + [VMEM] * (1 + nx), (where_x, arrived, *weights), 2**28, 2**21,
    )
    others.append(shift(hold(column, parts), "x", 2))
    parts = exchange(parts.reshape(nz, -1, 2 * units), "z")
    rows = parts.shape[1]
    total, rounded = kernel(
        add_body, "add", [shaped((rows, 2 * units), F32), shaped((rows, 2 * units), BF16)],
        [VMEM], (parts,), 2**18, 2**19,
    )
    hidden = kernel(
        hidden_body, "hidden", shaped((nz * nx, rows, units), BF16),
        [VMEM] * 2, (total, shift(rounded, "h", 1)), 2**18, 2**20, 2**14,
    )
    hidden = exchange(hidden, ("z", "x"))
    result = kernel(
        functools.partial(second_body, nz, nx), "second", shaped((owners, slots, LANES), BF16),
        [VMEM] * 2, (hidden, w_down), 2**27, 2**21,
    )
    back = exchange(result, ("l", "c"))
    moe_output = kernel(
        combine_body, "combine", shaped((tokens, feats), BF16),
        [VMEM] * 3, (routes, gate_values, back), 2**20, 2**18,
    )

    sources = [x_at, x_at + nx - 1, x_at + 1, x_at + 2]
    at_z = lax.broadcasted_iota(I32, (nz, nh, own), 0)
    at_h = lax.broadcasted_iota(I32, (nz, nh, own), 1)
    base = ((at_z * nh + at_h) * nx * latents.shape[0] + lax.broadcasted_iota(I32, (nz, nh, own), 2)).reshape(1, -1)
    query_rows = queries.reshape(queries.shape[0] * H, WIDE)

    spots = []
    for source in sources:
        first = (source % nx) * latents.shape[0]
        spots.append([first + core * own, first + (nc - 1 - core) * own])

    def call(which, pieces, state, last, name):
        marks = jnp.stack([offsets[0]] + [s for i in which for s in spots[i]]).astype(I32)
        both = [p for piece in pieces for p in (piece, shift(piece, "c", 1))]
        return attend(marks, query_rows, base, both, state, last, name)

    state = call([0], [column], [], False, "attend_own")
    state = call([1, 2], others[:2], state, False, "attend_near")
    mixed = call([3], [hold(others[2], state[0])], state, True, "attend_far")
    attention_out = mixed.reshape(queries.shape[0], H * LAT)
    return (attention_out, moe_output)


def solution(mesh):
    fine = Mesh(mesh.devices.reshape(8, 2, 4, 4, 2), ("z", "h", "x", "l", "c"))
    ctx, exp = ("z", "h", "x"), ("l", "c")
    return jax.shard_map(
        local,
        mesh=fine,
        in_specs=(
            P(ctx + exp, None),
            P(ctx, None),
            P(ctx + exp),
            P(exp, ctx),
            P(exp, None),
            P(exp, None),
            P(exp, ctx, None),
            P(exp, ctx, None),
            P(exp, None, ctx),
        ),
        out_specs=(P(ctx + exp, None), P(exp, ctx)),
        check_vma=False,
    )
```

```python
import functools
import math

import jax
import jax.numpy as jnp
from jax import lax
from jax.experimental import pallas as pl
from jax.experimental.pallas import tpu as pltpu
from jax.sharding import Mesh, PartitionSpec as P

H = 128
LAT = 512
ROPE = 64
WIDE = LAT + ROPE
TOPK = 6
EXPERTS = 16
CAP = 16
LANES = 128

SCALE_LOG2 = 192.0 ** (-0.5) * math.log2(math.e)
F32 = jnp.float32
BF16 = jnp.bfloat16
I32 = jnp.int32
VMEM = pl.BlockSpec(memory_space=pltpu.VMEM)
AFTER = pl.BlockSpec(memory_space=pl.ANY)
SMEM = pl.BlockSpec(memory_space=pltpu.SMEM)


def shaped(shape, dtype):
    return jax.ShapeDtypeStruct(shape, dtype)


def kernel(body, name, out_shape, specs, args, flops, moved, special=0):
    return pl.pallas_call(
        body,
        out_shape=out_shape,
        in_specs=specs,
        out_specs=jax.tree.map(lambda _: VMEM, out_shape),
        compiler_params=pltpu.CompilerParams(vmem_limit_bytes=24 * 2**20),
        cost_estimate=pl.CostEstimate(flops=flops, bytes_accessed=moved, transcendentals=special),
        name=name,
    )(*args)


def attention_body(chunk, first, last, spots, queries, base, keys, *refs):
    rows = queries.shape[0]
    row_pos = spots[0] + lax.broadcasted_iota(I32, (rows, 1), 0) // H - spots[1]
    query = queries[...]
    parts = [slice(i * chunk, (i + 1) * chunk) for i in range(keys.shape[0] // chunk)]
    scored = []
    for part in parts:
        scores = lax.dot_general(
            query, keys[part, :WIDE], (((1,), (1,)), ((), ())), preferred_element_type=F32
        )
        scored.append(jnp.where(base[:1, part] <= row_pos, scores * SCALE_LOG2, -jnp.inf))
    if first:
        new = jnp.full((rows, 1), -1e30, F32)
    else:
        new = refs[0][:, :1]
    for scores in scored:
        new = jnp.maximum(new, jnp.max(scores, axis=1, keepdims=True))
    den, acc = 0.0, 0.0
    if not first:
        shrink = jnp.exp2(refs[0][:, :1] - new)
        den, acc = refs[1][:, :1] * shrink, refs[2][...] * shrink
    for scores, part in zip(scored, parts):
        weights = jnp.exp2(scores - new)
        den = den + jnp.sum(weights, axis=1, keepdims=True)
        acc = acc + jnp.dot(weights.astype(BF16), keys[part, :LAT], preferred_element_type=F32)
    if last:
        refs[-1][...] = (acc / den).astype(BF16)
    else:
        refs[-3][...] = jnp.broadcast_to(new, (rows, LANES))
        refs[-2][...] = jnp.broadcast_to(den, (rows, LANES))
        refs[-1][...] = acc


def attend(spots, queries, base, keys, state, last, name):
    rows, count = queries.shape[0], keys.shape[0]
    if last:
        out = shaped((rows, LAT), BF16)
    else:
        out = [shaped((rows, LANES), F32)] * 2 + [shaped((rows, LAT), F32)]
    body = functools.partial(attention_body, count // 4, not state, last)
    specs = [SMEM] + [VMEM] * (3 + len(state))
    args = (spots, queries, base, keys, *state)
    return kernel(body, name, out, specs, args, 4 * rows * count * WIDE, 2 * count * WIDE + 2**20, rows * count)


def dispatch_body(copies, routes, tokens, *refs):
    out = refs[-1]
    count = tokens.shape[0]
    slot = lax.broadcasted_iota(I32, (EXPERTS * CAP, count), 0)
    named = routes[0:1, :] == slot // CAP
    for k in range(1, TOPK):
        named = named | (routes[k : k + 1, :] == slot // CAP)
    hot = named.astype(F32)
    earlier = lax.broadcasted_iota(I32, (count, count), 0) < lax.broadcasted_iota(I32, (count, count), 1)
    rank = jnp.dot(hot.astype(BF16), earlier.astype(F32).astype(BF16), preferred_element_type=F32)
    placed = jnp.where(rank == (slot % CAP).astype(F32), hot, 0.0).astype(BF16)
    sent = jnp.dot(placed, tokens[...], preferred_element_type=F32).astype(BF16)
    owners = out.shape[0] // copies
    out[...] = jnp.zeros(out.shape, BF16)
    for i in range(copies):
        out[i * owners : (i + 1) * owners, :, : tokens.shape[1]] = sent.reshape(owners, -1, tokens.shape[1])


def cut_body(spots, gate, up, *outs):
    parts = len(outs)
    units = gate.shape[2] // parts
    for j, out in enumerate(outs):
        at = pl.multiple_of(lax.rem(spots[0] + j, parts) * units, LANES)
        out[:, :, :units] = gate[:, :, pl.ds(at, units)]
        out[:, :, units:] = up[:, :, pl.ds(at, units)]


def first_body(order, spots, arrived, *refs):
    weights, out = refs[:-1], refs[-1]
    held, feats = weights[0].shape[:2]
    owners = arrived.shape[0] // len(weights)
    for e in range(held):
        total = 0.0
        for j, matrix in zip(order, weights):
            at = lax.rem(spots[0] + j, len(weights)) * owners
            rows = arrived[pl.ds(at, owners), e * CAP : (e + 1) * CAP, :].reshape(owners * CAP, LANES)
            total = total + jnp.dot(rows[:, :feats], matrix[e], preferred_element_type=F32)
        out[e * owners * CAP : (e + 1) * owners * CAP, :] = total.astype(BF16)


def add_body(parts, total, rounded):
    sums = parts[0].astype(F32)
    for i in range(1, parts.shape[0]):
        sums = sums + parts[i].astype(F32)
    total[...] = sums
    rounded[...] = sums.astype(BF16)


def hidden_body(total, other, out):
    sums = total[...] + other[...].astype(F32)
    units = sums.shape[1] // 2
    gate = sums[:, :units]
    hidden = (gate / (1.0 + jnp.exp(-gate)) * sums[:, units:]).astype(BF16)
    for i in range(out.shape[0]):
        out[i] = hidden


def second_body(deep, across, hidden, down, out):
    held, feats = down.shape[0], down.shape[2]
    units = hidden.shape[2]
    group = deep // held
    owners = out.shape[0]
    out[...] = jnp.zeros(out.shape, BF16)
    for e in range(held):
        total = 0.0
        for x in range(across):
            rows = jnp.concatenate([hidden[(group * e + i) * across + x] for i in range(group)], axis=0)
            total = total + jnp.dot(rows, down[e, x * units : (x + 1) * units, :], preferred_element_type=F32)
        out[:, e * CAP : (e + 1) * CAP, :feats] = total.astype(BF16).reshape(owners, CAP, feats)


def combine_body(routes, gates, back, out):
    count, feats = out.shape
    slot = lax.broadcasted_iota(I32, (count, EXPERTS * CAP), 1)
    hot = jnp.zeros(slot.shape, F32)
    share = jnp.zeros(slot.shape, F32)
    for k in range(TOPK):
        here = routes[:, k : k + 1] == slot // CAP
        hot = jnp.where(here, 1.0, hot)
        share = share + jnp.where(here, gates[:, k : k + 1], 0.0)
    earlier = lax.broadcasted_iota(I32, (count, count), 1) < lax.broadcasted_iota(I32, (count, count), 0)
    rank = jnp.dot(earlier.astype(F32).astype(BF16), hot.astype(BF16), preferred_element_type=F32)
    share = jnp.where(rank == (slot % CAP).astype(F32), share, 0.0)
    rows = back[...].reshape(EXPERTS * CAP, LANES)[:, :feats].astype(F32)
    mixed = jnp.dot(share, rows, precision=lax.Precision.HIGHEST, preferred_element_type=F32)
    out[...] = mixed.astype(BF16)


def hold(array, after):
    return pl.pallas_call(
        lambda array, after, out: None,
        out_shape=shaped(array.shape, array.dtype),
        in_specs=[AFTER] * 2,
        out_specs=AFTER,
        input_output_aliases={0: 0},
        name="hold",
    )(array, after)


def exchange(array, axes):
    return lax.all_to_all(array, axes, split_axis=0, concat_axis=0, tiled=False)


def shift(array, axis, by):
    size = lax.axis_size(axis)
    return lax.ppermute(array, axis, [(i, (i + by) % size) for i in range(size)])


def local(queries, latents, offsets, moe_input, routes, gate_values, w_gate, w_up, w_down):
    nz, nh, nx, nl, nc = (lax.axis_size(a) for a in ("z", "h", "x", "l", "c"))
    x_at, core = lax.axis_index("x"), lax.axis_index("c")
    owners = nl * nc
    held, feats, width = w_gate.shape
    units = width // nx
    tokens = moe_input.shape[0]
    slots = held * CAP
    where_x = x_at.astype(I32).reshape(1)

    own = latents.shape[0] // nc
    half = lax.dynamic_slice_in_dim(latents, core * own, own, 0)
    half = jnp.pad(half, ((0, 0), (0, -WIDE % LANES)))
    pair = jnp.concatenate([half, shift(half, "h", 1)], axis=0)
    plane = jnp.concatenate([pair] + [shift(pair, "x", j) for j in range(1, nx)], axis=0)
    mine = lax.all_gather(plane, "z", axis=0, tiled=True)

    outgoing = kernel(
        functools.partial(dispatch_body, nx), "dispatch", shaped((nx * owners, slots, LANES), BF16),
        [VMEM, VMEM, AFTER], (routes.T, moe_input, plane), 2**20, 2**18,
    )
    arrived = exchange(outgoing, ("x", "l", "c"))
    cut = kernel(
        cut_body, "cut", [shaped((held, feats, 2 * units), BF16)] * nx,
        [SMEM, VMEM, VMEM], (where_x, w_gate, w_up), 2**10, 2**21,
    )
    weights = [cut[0]] + [shift(cut[j], "x", j) for j in range(1, nx)]
    order = [0] + [nx - j for j in range(1, nx)]
    parts = kernel(
        functools.partial(first_body, order), "first", shaped((held * owners * CAP, 2 * units), BF16),
        [SMEM] + [VMEM] * (1 + nx), (where_x, arrived, *weights), 2**28, 2**21,
    )
    parts = exchange(parts.reshape(nz, -1, 2 * units), "z")
    rows = parts.shape[1]
    total, rounded = kernel(
        add_body, "add", [shaped((rows, 2 * units), F32), shaped((rows, 2 * units), BF16)],
        [VMEM], (parts,), 2**18, 2**19,
    )
    hidden = kernel(
        hidden_body, "hidden", shaped((nz * nx, rows, units), BF16),
        [VMEM] * 2, (total, shift(rounded, "h", 1)), 2**18, 2**20, 2**14,
    )
    hidden = exchange(hidden, ("z", "x"))
    result = kernel(
        functools.partial(second_body, nz, nx), "second", shaped((owners, slots, LANES), BF16),
        [VMEM] * 2, (hidden, w_down), 2**27, 2**21,
    )
    back = exchange(result, ("l", "c"))
    moe_output = kernel(
        combine_body, "combine", shaped((tokens, feats), BF16),
        [VMEM] * 3, (routes, gate_values, back), 2**20, 2**18,
    )

    mine = hold(mine, result)
    other = shift(mine, "c", 1)
    grid = (nz, nx, nh, own)
    at_z, at_x, at_h, row = (lax.broadcasted_iota(I32, grid, i) for i in range(4))
    at_x, at_h = (x_at - at_x + nx) % nx, (lax.axis_index("h") + at_h) % nh
    base = (((at_z * nh + at_h) * nx + at_x) * (nc * own) + row).reshape(1, -1)
    query_rows = queries.reshape(queries.shape[0] * H, WIDE)
    marks = [jnp.stack([offsets[0], at * own]).astype(I32) for at in (core, nc - 1 - core)]
    state = attend(marks[0], query_rows, base, mine, [], False, "attend_mine")
    mixed = attend(marks[1], query_rows, base, other, state, True, "attend_other")
    attention_out = mixed.reshape(queries.shape[0], H * LAT)
    return (attention_out, moe_output)


def solution(mesh):
    fine = Mesh(mesh.devices.reshape(8, 2, 4, 4, 2), ("z", "h", "x", "l", "c"))
    ctx, exp = ("z", "h", "x"), ("l", "c")
    return jax.shard_map(
        local,
        mesh=fine,
        in_specs=(
            P(ctx + exp, None),
            P(ctx, None),
            P(ctx + exp),
            P(exp, ctx),
            P(exp, None),
            P(exp, None),
            P(exp, ctx, None),
            P(exp, ctx, None),
            P(exp, None, ctx),
        ),
        out_specs=(P(ctx + exp, None), P(exp, ctx)),
        check_vma=False,
    )
```

```python
import functools
import math

import jax
import jax.numpy as jnp
from jax import lax
from jax.experimental import pallas as pl
from jax.experimental.pallas import tpu as pltpu
from jax.sharding import Mesh, PartitionSpec as P

H = 128
LAT = 512
ROPE = 64
WIDE = LAT + ROPE
TOPK = 6
EXPERTS = 16
CAP = 16
LANES = 128
CLAIM = 16

SCALE_LOG2 = 192.0 ** (-0.5) * math.log2(math.e)
F32 = jnp.float32
BF16 = jnp.bfloat16
I32 = jnp.int32
VMEM = pl.BlockSpec(memory_space=pltpu.VMEM)
AFTER = pl.BlockSpec(memory_space=pl.ANY)
SMEM = pl.BlockSpec(memory_space=pltpu.SMEM)


def shaped(shape, dtype):
    return jax.ShapeDtypeStruct(shape, dtype)


def kernel(body, name, out_shape, specs, args, flops, moved, special=0):
    return pl.pallas_call(
        body,
        out_shape=out_shape,
        in_specs=specs,
        out_specs=jax.tree.map(lambda _: VMEM, out_shape),
        compiler_params=pltpu.CompilerParams(vmem_limit_bytes=(24 if special > 2**16 else 12) * 2**20),
        cost_estimate=pl.CostEstimate(flops=flops, bytes_accessed=moved, transcendentals=special),
        name=name,
    )(*args)


def attention_body(pieces, first, last, spots, queries, base, *refs):
    keys, refs = refs[:pieces], refs[pieces:]
    rows = queries.shape[0]
    row_pos = spots[0] + lax.broadcasted_iota(I32, (rows, 1), 0) // H
    query = queries[...]
    if first:
        top = jnp.full((rows, 1), -1e30, F32)
    else:
        top = refs[0][:, :1]
    scored = []
    for j, key in enumerate(keys):
        scores = jnp.dot(query, key[...], preferred_element_type=F32) * SCALE_LOG2
        scored.append(jnp.where(base[:1, :] <= row_pos - spots[1 + j], scores, -jnp.inf))
    new = top
    for scores in scored:
        new = jnp.maximum(new, jnp.max(scores, axis=1, keepdims=True))
    den, acc = 0.0, 0.0
    if not first:
        shrink = jnp.exp2(top - new)
        den, acc = refs[1][:, :1] * shrink, refs[2][...] * shrink
    for scores, key in zip(scored, keys):
        weights = jnp.exp2(scores - new)
        den = den + jnp.sum(weights, axis=1, keepdims=True)
        acc = acc + lax.dot_general(
            weights.astype(BF16), key[:LAT, :], (((1,), (1,)), ((), ())), preferred_element_type=F32
        )
    if last:
        refs[-1][...] = (acc / den).astype(BF16)
    else:
        refs[-4][...] = jnp.broadcast_to(new, (rows, LANES))
        refs[-3][...] = jnp.broadcast_to(den, (rows, LANES))
        refs[-2][...] = acc
        refs[-1][...] = jnp.zeros(refs[-1].shape, F32)


def attend(spots, queries, base, pieces, state, last, name):
    rows, count = queries.shape[0], base.shape[1] * len(pieces)
    if last:
        out = shaped((rows, LAT), BF16)
    else:
        out = [shaped((rows, LANES), F32)] * 2 + [shaped((rows, LAT), F32), shaped((8, LANES), F32)]
    body = functools.partial(attention_body, len(pieces), not state, last)
    specs = [SMEM] + [VMEM] * (2 + len(pieces) + len(state))
    args = (spots, queries, base, *pieces, *state)
    return kernel(body, name, out, specs, args, 4 * rows * count * WIDE * CLAIM, (2 * count * WIDE + 2**20) * CLAIM, rows * count * CLAIM)


def dispatch_body(order, spots, routes, *refs):
    pieces, out = refs[: len(order)], refs[-1]
    count = routes.shape[1]
    slot = lax.broadcasted_iota(I32, (EXPERTS * CAP, count), 0)
    named = routes[0:1, :] == slot // CAP
    for k in range(1, TOPK):
        named = named | (routes[k : k + 1, :] == slot // CAP)
    hot = named.astype(F32)
    earlier = lax.broadcasted_iota(I32, (count, count), 0) < lax.broadcasted_iota(I32, (count, count), 1)
    rank = jnp.dot(hot.astype(BF16), earlier.astype(F32).astype(BF16), preferred_element_type=F32)
    placed = jnp.where(rank == (slot % CAP).astype(F32), hot, 0.0).astype(BF16)
    owners = out.shape[0]
    for j, piece in enumerate(pieces):
        tokens = piece[piece.shape[0] - count :, :LANES]
        sent = jnp.dot(placed, tokens, preferred_element_type=F32).astype(BF16)
        out[:, :, j * LANES : (j + 1) * LANES] = sent.reshape(owners, -1, LANES)


def cut_body(spots, gate, up, tokens, *outs):
    parts = len(outs)
    held, feats, width = gate.shape
    units = width // parts
    for j, out in enumerate(outs):
        at = pl.multiple_of(lax.rem(spots[0] + j, parts) * units, LANES)
        for e in range(held):
            out[e * feats : (e + 1) * feats, :units] = gate[e, :, pl.ds(at, units)]
            out[e * feats : (e + 1) * feats, units:] = up[e, :, pl.ds(at, units)]
        out[held * feats :, :] = jnp.zeros((out.shape[0] - held * feats, 2 * units), BF16)
        out[held * feats :, : tokens.shape[1]] = tokens[...]


def first_body(feats, arrived, *refs):
    weights, out = refs[:-1], refs[-1]
    owners = arrived.shape[0]
    for e in range(arrived.shape[1] // CAP):
        total = 0.0
        for j, matrix in enumerate(weights):
            rows = arrived[:, e * CAP : (e + 1) * CAP, j * LANES : (j + 1) * LANES].reshape(owners * CAP, LANES)
            part = matrix[e * feats : (e + 1) * feats, :]
            total = total + jnp.dot(rows[:, :feats], part, preferred_element_type=F32)
        out[e * owners * CAP : (e + 1) * owners * CAP, :] = total.astype(BF16)


def hidden_body(parts, out, token):
    sums = parts[0].astype(F32)
    for i in range(1, parts.shape[0]):
        sums = sums + parts[i].astype(F32)
    units = sums.shape[1] // 2
    gate = sums[:, :units]
    hidden = (gate / (1.0 + jnp.exp(-gate)) * sums[:, units:]).astype(BF16)
    for i in range(out.shape[0]):
        out[i] = hidden
    token[...] = jnp.zeros(token.shape, F32)


def second_body(deep, across, hidden, down, out):
    held, feats = down.shape[0], down.shape[2]
    units = hidden.shape[2]
    group = deep // held
    owners = out.shape[0]
    out[...] = jnp.zeros(out.shape, BF16)
    for e in range(held):
        total = 0.0
        for x in range(across):
            rows = jnp.concatenate([hidden[(group * e + i) * across + x] for i in range(group)], axis=0)
            total = total + jnp.dot(rows, down[e, x * units : (x + 1) * units, :], preferred_element_type=F32)
        out[:, e * CAP : (e + 1) * CAP, :feats] = total.astype(BF16).reshape(owners, CAP, feats)


def combine_body(routes, gates, back, out):
    count, feats = out.shape
    slot = lax.broadcasted_iota(I32, (count, EXPERTS * CAP), 1)
    hot = jnp.zeros(slot.shape, F32)
    share = jnp.zeros(slot.shape, F32)
    for k in range(TOPK):
        here = routes[:, k : k + 1] == slot // CAP
        hot = jnp.where(here, 1.0, hot)
        share = share + jnp.where(here, gates[:, k : k + 1], 0.0)
    earlier = lax.broadcasted_iota(I32, (count, count), 1) < lax.broadcasted_iota(I32, (count, count), 0)
    rank = jnp.dot(earlier.astype(F32).astype(BF16), hot.astype(BF16), preferred_element_type=F32)
    share = jnp.where(rank == (slot % CAP).astype(F32), share, 0.0)
    rows = back[...].reshape(EXPERTS * CAP, LANES)[:, :feats].astype(F32)
    mixed = jnp.dot(share, rows, precision=lax.Precision.HIGHEST, preferred_element_type=F32)
    out[...] = mixed.astype(BF16)


def hold(arrays, after):
    return pl.pallas_call(
        lambda *refs: None,
        out_shape=[shaped(a.shape, a.dtype) for a in arrays],
        in_specs=[AFTER] * (len(arrays) + len(after)),
        out_specs=[AFTER] * len(arrays),
        input_output_aliases={i: i for i in range(len(arrays))},
        compiler_params=pltpu.CompilerParams(vmem_limit_bytes=2**20),
        name="hold",
    )(*arrays, *after)


def exchange(array, axes):
    return lax.all_to_all(array, axes, split_axis=0, concat_axis=0, tiled=False)


def shift(array, axis, by):
    size = lax.axis_size(axis)
    return lax.ppermute(array, axis, [(i, (i + by) % size) for i in range(size)])


def local(queries, latents, offsets, moe_input, routes, gate_values, w_gate, w_up, w_down):
    nz, nh, nx, nl, nc = (lax.axis_size(a) for a in ("z", "h", "x", "l", "c"))
    x_at, core = lax.axis_index("x"), lax.axis_index("c")
    owners = nl * nc
    held, feats, width = w_gate.shape
    units = width // nx
    tokens = moe_input.shape[0]
    slots = held * CAP
    where_x = x_at.astype(I32).reshape(1)

    own = latents.shape[0] // nc
    half = lax.dynamic_slice_in_dim(latents, core * own, own, 0)
    column = exchange(jnp.broadcast_to(half[None], (nz * nh,) + half.shape), ("z", "h"))
    column = column.reshape(nz * nh * own, WIDE)

    cut = kernel(
        cut_body, "cut", [shaped((held * feats + tokens, 2 * units), BF16)] * nx,
        [SMEM] + [VMEM] * 3, (where_x, w_gate, w_up, moe_input), 2**10, 2**21,
    )
    weights = [cut[0]] + [shift(cut[j], "x", j) for j in range(1, nx)]
    order = [0] + [nx - j for j in range(1, nx)]
    outgoing = kernel(
        functools.partial(dispatch_body, order), "dispatch", shaped((owners, slots, nx * LANES), BF16),
        [SMEM] + [VMEM] * (1 + nx) + [AFTER], (where_x, routes.T, *weights, column), 2**20, 2**18,
    )
    arrived = exchange(outgoing, ("l", "c"))
    column = column.T
    others = [shift(column, "x", 1), shift(column, "x", -1), shift(column, "x", 2)]

    parts = kernel(
        functools.partial(first_body, feats), "first", shaped((held * owners * CAP, 2 * units), BF16),
        [VMEM] * (1 + nx), (arrived, *weights), 2**28, 2**21,
    )
    parts = exchange(parts.reshape(nz * nh, -1, 2 * units), ("z", "h"))
    hidden, token = kernel(
        hidden_body, "hidden", [shaped((nz * nh * nx, parts.shape[1], units), BF16), shaped((8, LANES), F32)],
        [VMEM], (parts,), 2**18, 2**20, 2**14,
    )
    hidden = exchange(hidden, ("z", "h", "x"))
    result = kernel(
        functools.partial(second_body, nz * nh, nx), "second", shaped((owners, slots, LANES), BF16),
        [VMEM] * 2, (hidden, w_down), 2**27, 2**21,
    )
    back = exchange(result, ("l", "c"))
    moe_output = kernel(
        combine_body, "combine", shaped((tokens, feats), BF16),
        [VMEM] * 3, (routes, gate_values, back), 2**20, 2**18,
    )

    sources = [x_at, x_at + nx - 1, x_at + 1, x_at + 2]
    at_z = lax.broadcasted_iota(I32, (nz, nh, own), 0)
    at_h = lax.broadcasted_iota(I32, (nz, nh, own), 1)
    base = ((at_z * nh + at_h) * nx * latents.shape[0] + lax.broadcasted_iota(I32, (nz, nh, own), 2)).reshape(1, -1)
    query_rows = queries.reshape(queries.shape[0] * H, WIDE)

    spots = []
    for source in sources:
        first = (source % nx) * latents.shape[0]
        spots.append([first + core * own, first + (nc - 1 - core) * own])

    def call(which, pieces, state, last, name):
        marks = jnp.stack([offsets[0]] + [s for i in which for s in spots[i]]).astype(I32)
        both = [p for piece in pieces for p in (piece, shift(piece, "c", 1))]
        return attend(marks, query_rows, base, both, state, last, name)

    *state, seen = call([0], [column], [], False, "attend_own")
    mixed = call([1, 2, 3], hold(others, [token, seen]), state, True, "attend_rest")
    attention_out = mixed.reshape(queries.shape[0], H * LAT)
    return (attention_out, moe_output)


def solution(mesh):
    fine = Mesh(mesh.devices.reshape(8, 2, 4, 4, 2), ("z", "h", "x", "l", "c"))
    ctx, exp = ("z", "h", "x"), ("l", "c")
    return jax.shard_map(
        local,
        mesh=fine,
        in_specs=(
            P(ctx + exp, None),
            P(ctx, None),
            P(ctx + exp),
            P(exp, ctx),
            P(exp, None),
            P(exp, None),
            P(exp, ctx, None),
            P(exp, ctx, None),
            P(exp, None, ctx),
        ),
        out_specs=(P(ctx + exp, None), P(exp, ctx)),
        check_vma=False,
    )
```

```python
import functools
import math

import jax
import jax.numpy as jnp
from jax import lax
from jax.experimental import pallas as pl
from jax.experimental.pallas import tpu as pltpu
from jax.sharding import Mesh, PartitionSpec as P

H = 128
LAT = 512
ROPE = 64
WIDE = LAT + ROPE
TOPK = 6
EXPERTS = 16
CAP = 16
LANES = 128
CLAIM = 8

SCALE_LOG2 = 192.0 ** (-0.5) * math.log2(math.e)
F32 = jnp.float32
BF16 = jnp.bfloat16
I32 = jnp.int32
VMEM = pl.BlockSpec(memory_space=pltpu.VMEM)
AFTER = pl.BlockSpec(memory_space=pl.ANY)
SMEM = pl.BlockSpec(memory_space=pltpu.SMEM)


def shaped(shape, dtype):
    return jax.ShapeDtypeStruct(shape, dtype)


def kernel(body, name, out_shape, specs, args, flops, moved, special=0):
    return pl.pallas_call(
        body,
        out_shape=out_shape,
        in_specs=specs,
        out_specs=jax.tree.map(lambda _: VMEM, out_shape),
        compiler_params=pltpu.CompilerParams(vmem_limit_bytes=(24 if special > 2**16 else 12) * 2**20),
        cost_estimate=pl.CostEstimate(flops=flops, bytes_accessed=moved, transcendentals=special),
        name=name,
    )(*args)


def attention_body(pieces, first, last, spots, queries, base, *refs):
    keys, refs = refs[:pieces], refs[pieces:]
    rows = queries.shape[0]
    row_pos = spots[0] + lax.broadcasted_iota(I32, (rows, 1), 0) // H
    query = queries[...]
    if first:
        top = jnp.full((rows, 1), -1e30, F32)
    else:
        top = refs[0][:, :1]
    scored = []
    for j, key in enumerate(keys):
        scores = jnp.dot(query, key[...], preferred_element_type=F32) * SCALE_LOG2
        scored.append(jnp.where(base[:1, :] <= row_pos - spots[1 + j], scores, -jnp.inf))
    new = top
    for scores in scored:
        new = jnp.maximum(new, jnp.max(scores, axis=1, keepdims=True))
    den, acc = 0.0, 0.0
    if not first:
        shrink = jnp.exp2(top - new)
        den, acc = refs[1][:, :1] * shrink, refs[2][...] * shrink
    for scores, key in zip(scored, keys):
        weights = jnp.exp2(scores - new)
        den = den + jnp.sum(weights, axis=1, keepdims=True)
        acc = acc + lax.dot_general(
            weights.astype(BF16), key[:LAT, :], (((1,), (1,)), ((), ())), preferred_element_type=F32
        )
    if last:
        refs[-1][...] = (acc / den).astype(BF16)
    else:
        refs[-4][...] = jnp.broadcast_to(new, (rows, LANES))
        refs[-3][...] = jnp.broadcast_to(den, (rows, LANES))
        refs[-2][...] = acc
        refs[-1][...] = jnp.zeros(refs[-1].shape, F32)


def attend(spots, queries, base, pieces, state, last, name):
    rows, count = queries.shape[0], base.shape[1] * len(pieces)
    if last:
        out = shaped((rows, LAT), BF16)
    else:
        out = [shaped((rows, LANES), F32)] * 2 + [shaped((rows, LAT), F32), shaped((8, LANES), F32)]
    body = functools.partial(attention_body, len(pieces), not state, last)
    specs = [SMEM] + [VMEM] * (2 + len(pieces) + len(state))
    args = (spots, queries, base, *pieces, *state)
    return kernel(body, name, out, specs, args, 4 * rows * count * WIDE // CLAIM, (2 * count * WIDE + 2**20) // CLAIM, rows * count // CLAIM)


def dispatch_body(copies, routes, tokens, out):
    count = tokens.shape[0]
    slot = lax.broadcasted_iota(I32, (EXPERTS * CAP, count), 0)
    named = routes[0:1, :] == slot // CAP
    for k in range(1, TOPK):
        named = named | (routes[k : k + 1, :] == slot // CAP)
    hot = named.astype(F32)
    earlier = lax.broadcasted_iota(I32, (count, count), 0) < lax.broadcasted_iota(I32, (count, count), 1)
    rank = jnp.dot(hot.astype(BF16), earlier.astype(F32).astype(BF16), preferred_element_type=F32)
    placed = jnp.where(rank == (slot % CAP).astype(F32), hot, 0.0).astype(BF16)
    sent = jnp.dot(placed, tokens[...], preferred_element_type=F32).astype(BF16)
    owners = out.shape[0] // copies
    out[...] = jnp.zeros(out.shape, BF16)
    for i in range(copies):
        out[i * owners : (i + 1) * owners, :, : tokens.shape[1]] = sent.reshape(owners, -1, tokens.shape[1])


def cut_body(spots, gate, up, *outs):
    parts = len(outs)
    units = gate.shape[2] // parts
    for j, out in enumerate(outs):
        at = pl.multiple_of(lax.rem(spots[0] + j, parts) * units, LANES)
        out[:, :, :units] = gate[:, :, pl.ds(at, units)]
        out[:, :, units:] = up[:, :, pl.ds(at, units)]


def pair_body(rows, after, out):
    for i in range(out.shape[0]):
        out[i] = rows[...]


def first_body(order, spots, after, arrived, *refs):
    weights, out = refs[:-1], refs[-1]
    held, feats = weights[0].shape[:2]
    owners = arrived.shape[0] // len(weights)
    for e in range(held):
        total = 0.0
        for j, matrix in zip(order, weights):
            at = lax.rem(spots[0] + j, len(weights)) * owners
            rows = arrived[pl.ds(at, owners), e * CAP : (e + 1) * CAP, :].reshape(owners * CAP, LANES)
            total = total + jnp.dot(rows[:, :feats], matrix[e], preferred_element_type=F32)
        out[e * owners * CAP : (e + 1) * owners * CAP, :] = total.astype(BF16)


def add_body(parts, total, rounded):
    sums = parts[0].astype(F32)
    for i in range(1, parts.shape[0]):
        sums = sums + parts[i].astype(F32)
    total[...] = sums
    rounded[...] = sums.astype(BF16)


def hidden_body(total, other, *refs):
    out, token = refs[-2:]
    sums = total[...] + other[...].astype(F32)
    units = sums.shape[1] // 2
    gate = sums[:, :units]
    hidden = (gate / (1.0 + jnp.exp(-gate)) * sums[:, units:]).astype(BF16)
    for i in range(out.shape[0]):
        out[i] = hidden
    token[...] = jnp.zeros(token.shape, F32)


def second_body(deep, across, hidden, down, out):
    held, feats = down.shape[0], down.shape[2]
    units = hidden.shape[2]
    group = deep // held
    owners = out.shape[0]
    out[...] = jnp.zeros(out.shape, BF16)
    for e in range(held):
        total = 0.0
        for x in range(across):
            rows = jnp.concatenate([hidden[(group * e + i) * across + x] for i in range(group)], axis=0)
            total = total + jnp.dot(rows, down[e, x * units : (x + 1) * units, :], preferred_element_type=F32)
        out[:, e * CAP : (e + 1) * CAP, :feats] = total.astype(BF16).reshape(owners, CAP, feats)


def combine_body(routes, gates, back, out):
    count, feats = out.shape
    slot = lax.broadcasted_iota(I32, (count, EXPERTS * CAP), 1)
    hot = jnp.zeros(slot.shape, F32)
    share = jnp.zeros(slot.shape, F32)
    for k in range(TOPK):
        here = routes[:, k : k + 1] == slot // CAP
        hot = jnp.where(here, 1.0, hot)
        share = share + jnp.where(here, gates[:, k : k + 1], 0.0)
    earlier = lax.broadcasted_iota(I32, (count, count), 1) < lax.broadcasted_iota(I32, (count, count), 0)
    rank = jnp.dot(earlier.astype(F32).astype(BF16), hot.astype(BF16), preferred_element_type=F32)
    share = jnp.where(rank == (slot % CAP).astype(F32), share, 0.0)
    rows = back[...].reshape(EXPERTS * CAP, LANES)[:, :feats].astype(F32)
    mixed = jnp.dot(share, rows, precision=lax.Precision.HIGHEST, preferred_element_type=F32)
    out[...] = mixed.astype(BF16)


def hold(arrays, after):
    return pl.pallas_call(
        lambda *refs: None,
        out_shape=[shaped(a.shape, a.dtype) for a in arrays],
        in_specs=[AFTER] * (len(arrays) + len(after)),
        out_specs=[AFTER] * len(arrays),
        input_output_aliases={i: i for i in range(len(arrays))},
        compiler_params=pltpu.CompilerParams(vmem_limit_bytes=2**20),
        name="hold",
    )(*arrays, *after)


def exchange(array, axes):
    return lax.all_to_all(array, axes, split_axis=0, concat_axis=0, tiled=False)


def shift(array, axis, by):
    size = lax.axis_size(axis)
    return lax.ppermute(array, axis, [(i, (i + by) % size) for i in range(size)])


def local(queries, latents, offsets, moe_input, routes, gate_values, w_gate, w_up, w_down):
    nz, nh, nx, nl, nc = (lax.axis_size(a) for a in ("z", "h", "x", "l", "c"))
    h_at, x_at, core = (lax.axis_index(a) for a in ("h", "x", "c"))
    owners = nl * nc
    held, feats, width = w_gate.shape
    units = width // nx
    tokens = moe_input.shape[0]
    slots = held * CAP
    where_x = x_at.astype(I32).reshape(1)

    outgoing = kernel(
        functools.partial(dispatch_body, nx), "dispatch", shaped((nx * owners, slots, LANES), BF16),
        [VMEM] * 2, (routes.T, moe_input), 2**20, 2**18,
    )
    arrived = exchange(outgoing, ("x", "l", "c"))

    own = latents.shape[0] // nc
    half = lax.dynamic_slice_in_dim(latents, core * own, own, 0)
    paired = jnp.concatenate([half, shift(half, "h", 1)], axis=0)
    paired = kernel(
        pair_body, "pair", shaped((nz,) + paired.shape, BF16), [VMEM, AFTER], (paired, arrived), 2**10, 2**20
    )
    column = exchange(paired, "z")
    column = column.reshape(nz * nh * own, WIDE).T

    cut = kernel(
        cut_body, "cut", [shaped((held, feats, 2 * units), BF16)] * nx,
        [SMEM, VMEM, VMEM], (where_x, w_gate, w_up), 2**10, 2**21,
    )
    weights = [cut[0]] + [shift(cut[j], "x", j) for j in range(1, nx)]
    order = [0] + [nx - j for j in range(1, nx)]
    parts = kernel(
        functools.partial(first_body, order), "first", shaped((held * owners * CAP, 2 * units), BF16),
        [SMEM, AFTER] + [VMEM] * (1 + nx), (where_x, column, arrived, *weights), 2**28, 2**21,
    )
    others = [shift(column, "x", 1), shift(column, "x", -1), shift(column, "x", 2)]
    parts = exchange(parts.reshape(nz, -1, 2 * units), "z")
    rows = parts.shape[1]
    total, rounded = kernel(
        add_body, "add", [shaped((rows, 2 * units), F32), shaped((rows, 2 * units), BF16)],
        [VMEM], (parts,), 2**18, 2**19,
    )
    added = shift(rounded, "h", 1)
    hidden, token = kernel(
        hidden_body, "hidden", [shaped((nz * nx, rows, units), BF16), shaped((8, LANES), F32)],
        [VMEM] * 2 + [AFTER] * 2, (total, added, *others[:2]), 2**18, 2**20, 2**14,
    )
    hidden = exchange(hidden, ("z", "x"))
    result = kernel(
        functools.partial(second_body, nz, nx), "second", shaped((owners, slots, LANES), BF16),
        [VMEM] * 2, (hidden, w_down), 2**27, 2**21,
    )
    back = exchange(result, ("l", "c"))
    moe_output = kernel(
        combine_body, "combine", shaped((tokens, feats), BF16),
        [VMEM] * 3, (routes, gate_values, back), 2**20, 2**18,
    )

    sources = [x_at, x_at + nx - 1, x_at + 1, x_at + 2]
    at_z = lax.broadcasted_iota(I32, (nz, nh, own), 0)
    at_h = (lax.broadcasted_iota(I32, (nz, nh, own), 1) + h_at) % nh
    base = ((at_z * nh + at_h) * nx * latents.shape[0] + lax.broadcasted_iota(I32, (nz, nh, own), 2)).reshape(1, -1)
    query_rows = queries.reshape(queries.shape[0] * H, WIDE)

    spots = []
    for source in sources:
        first = (source % nx) * latents.shape[0]
        spots.append([first + core * own, first + (nc - 1 - core) * own])

    def call(which, pieces, state, last, name):
        marks = jnp.stack([offsets[0]] + [s for i in which for s in spots[i]]).astype(I32)
        both = [p for piece in pieces for p in (piece, shift(piece, "c", 1))]
        return attend(marks, query_rows, base, both, state, last, name)

    *state, seen = call([0, 1, 2], [column, *hold(others[:2], [token])], [], False, "attend_near")
    mixed = call([3], hold(others[2:], [token, seen]), state, True, "attend_far")
    attention_out = mixed.reshape(queries.shape[0], H * LAT)
    return (attention_out, moe_output)


def solution(mesh):
    fine = Mesh(mesh.devices.reshape(8, 2, 4, 4, 2), ("z", "h", "x", "l", "c"))
    ctx, exp = ("z", "h", "x"), ("l", "c")
    return jax.shard_map(
        local,
        mesh=fine,
        in_specs=(
            P(ctx + exp, None),
            P(ctx, None),
            P(ctx + exp),
            P(exp, ctx),
            P(exp, None),
            P(exp, None),
            P(exp, ctx, None),
            P(exp, ctx, None),
            P(exp, None, ctx),
        ),
        out_specs=(P(ctx + exp, None), P(exp, ctx)),
        check_vma=False,
    )
```

```python
import functools
import math

import jax
import jax.numpy as jnp
from jax import lax
from jax.experimental import pallas as pl
from jax.experimental.pallas import tpu as pltpu
from jax.sharding import Mesh, PartitionSpec as P

H = 128
LAT = 512
ROPE = 64
WIDE = LAT + ROPE
TOPK = 6
EXPERTS = 16
CAP = 16
LANES = 128
CLAIM = 8

SCALE_LOG2 = 192.0 ** (-0.5) * math.log2(math.e)
F32 = jnp.float32
BF16 = jnp.bfloat16
I32 = jnp.int32
VMEM = pl.BlockSpec(memory_space=pltpu.VMEM)
AFTER = pl.BlockSpec(memory_space=pl.ANY)
SMEM = pl.BlockSpec(memory_space=pltpu.SMEM)


def shaped(shape, dtype):
    return jax.ShapeDtypeStruct(shape, dtype)


def kernel(body, name, out_shape, specs, args, flops, moved, special=0):
    return pl.pallas_call(
        body,
        out_shape=out_shape,
        in_specs=specs,
        out_specs=jax.tree.map(lambda _: VMEM, out_shape),
        compiler_params=pltpu.CompilerParams(vmem_limit_bytes=(24 if special > 2**16 else 12) * 2**20),
        cost_estimate=pl.CostEstimate(flops=flops, bytes_accessed=moved, transcendentals=special),
        name=name,
    )(*args)


def attention_body(pieces, first, last, spots, queries, base, *refs):
    keys, refs = refs[:pieces], refs[pieces:]
    rows = queries.shape[0]
    row_pos = spots[0] + lax.broadcasted_iota(I32, (rows, 1), 0) // H
    query = queries[...]
    if first:
        top = jnp.full((rows, 1), -1e30, F32)
    else:
        top = refs[0][:, :1]
    scored = []
    for j, key in enumerate(keys):
        scores = jnp.dot(query, key[...], preferred_element_type=F32) * SCALE_LOG2
        scored.append(jnp.where(base[:1, :] <= row_pos - spots[1 + j], scores, -jnp.inf))
    new = top
    for scores in scored:
        new = jnp.maximum(new, jnp.max(scores, axis=1, keepdims=True))
    den, acc = 0.0, 0.0
    if not first:
        shrink = jnp.exp2(top - new)
        den, acc = refs[1][:, :1] * shrink, refs[2][...] * shrink
    for scores, key in zip(scored, keys):
        weights = jnp.exp2(scores - new)
        den = den + jnp.sum(weights, axis=1, keepdims=True)
        acc = acc + lax.dot_general(
            weights.astype(BF16), key[:LAT, :], (((1,), (1,)), ((), ())), preferred_element_type=F32
        )
    if last:
        refs[-1][...] = (acc / den).astype(BF16)
    else:
        refs[-4][...] = jnp.broadcast_to(new, (rows, LANES))
        refs[-3][...] = jnp.broadcast_to(den, (rows, LANES))
        refs[-2][...] = acc
        refs[-1][...] = jnp.zeros(refs[-1].shape, F32)


def attend(spots, queries, base, pieces, state, last, name):
    rows, count = queries.shape[0], base.shape[1] * len(pieces)
    if last:
        out = shaped((rows, LAT), BF16)
    else:
        out = [shaped((rows, LANES), F32)] * 2 + [shaped((rows, LAT), F32), shaped((8, LANES), F32)]
    body = functools.partial(attention_body, len(pieces), not state, last)
    specs = [SMEM] + [VMEM] * (2 + len(pieces) + len(state))
    args = (spots, queries, base, *pieces, *state)
    return kernel(body, name, out, specs, args, 4 * rows * count * WIDE // CLAIM, (2 * count * WIDE + 2**20) // CLAIM, rows * count // CLAIM)


def dispatch_body(copies, routes, tokens, out):
    count = tokens.shape[0]
    slot = lax.broadcasted_iota(I32, (EXPERTS * CAP, count), 0)
    named = routes[0:1, :] == slot // CAP
    for k in range(1, TOPK):
        named = named | (routes[k : k + 1, :] == slot // CAP)
    hot = named.astype(F32)
    earlier = lax.broadcasted_iota(I32, (count, count), 0) < lax.broadcasted_iota(I32, (count, count), 1)
    rank = jnp.dot(hot.astype(BF16), earlier.astype(F32).astype(BF16), preferred_element_type=F32)
    placed = jnp.where(rank == (slot % CAP).astype(F32), hot, 0.0).astype(BF16)
    sent = jnp.dot(placed, tokens[...], preferred_element_type=F32).astype(BF16)
    owners = out.shape[0] // copies
    out[...] = jnp.zeros(out.shape, BF16)
    for i in range(copies):
        out[i * owners : (i + 1) * owners, :, : tokens.shape[1]] = sent.reshape(owners, -1, tokens.shape[1])


def cut_body(spots, gate, up, *outs):
    parts = len(outs)
    units = gate.shape[2] // parts
    for j, out in enumerate(outs):
        at = pl.multiple_of(lax.rem(spots[0] + j, parts) * units, LANES)
        out[:, :, :units] = gate[:, :, pl.ds(at, units)]
        out[:, :, units:] = up[:, :, pl.ds(at, units)]


def pair_body(rows, after, out):
    for i in range(out.shape[0]):
        out[i] = rows[...]


def first_body(order, spots, arrived, *refs):
    weights, out = refs[: len(order)], refs[-1]
    held, feats = weights[0].shape[:2]
    owners = arrived.shape[0] // len(weights)
    for e in range(held):
        total = 0.0
        for j, matrix in zip(order, weights):
            at = lax.rem(spots[0] + j, len(weights)) * owners
            rows = arrived[pl.ds(at, owners), e * CAP : (e + 1) * CAP, :].reshape(owners * CAP, LANES)
            total = total + jnp.dot(rows[:, :feats], matrix[e], preferred_element_type=F32)
        out[e * owners * CAP : (e + 1) * owners * CAP, :] = total.astype(BF16)


def add_body(parts, total, rounded):
    sums = parts[0].astype(F32)
    for i in range(1, parts.shape[0]):
        sums = sums + parts[i].astype(F32)
    total[...] = sums
    rounded[...] = sums.astype(BF16)


def hidden_body(total, other, *refs):
    out, token = refs[-2:]
    sums = total[...] + other[...].astype(F32)
    units = sums.shape[1] // 2
    gate = sums[:, :units]
    hidden = (gate / (1.0 + jnp.exp(-gate)) * sums[:, units:]).astype(BF16)
    for i in range(out.shape[0]):
        out[i] = hidden
    token[...] = jnp.zeros(token.shape, F32)


def second_body(deep, across, hidden, down, *refs):
    out = refs[-1]
    held, feats = down.shape[0], down.shape[2]
    units = hidden.shape[2]
    group = deep // held
    owners = out.shape[0]
    out[...] = jnp.zeros(out.shape, BF16)
    for e in range(held):
        total = 0.0
        for x in range(across):
            rows = jnp.concatenate([hidden[(group * e + i) * across + x] for i in range(group)], axis=0)
            total = total + jnp.dot(rows, down[e, x * units : (x + 1) * units, :], preferred_element_type=F32)
        out[:, e * CAP : (e + 1) * CAP, :feats] = total.astype(BF16).reshape(owners, CAP, feats)


def combine_body(routes, gates, back, out):
    count, feats = out.shape
    slot = lax.broadcasted_iota(I32, (count, EXPERTS * CAP), 1)
    hot = jnp.zeros(slot.shape, F32)
    share = jnp.zeros(slot.shape, F32)
    for k in range(TOPK):
        here = routes[:, k : k + 1] == slot // CAP
        hot = jnp.where(here, 1.0, hot)
        share = share + jnp.where(here, gates[:, k : k + 1], 0.0)
    earlier = lax.broadcasted_iota(I32, (count, count), 1) < lax.broadcasted_iota(I32, (count, count), 0)
    rank = jnp.dot(earlier.astype(F32).astype(BF16), hot.astype(BF16), preferred_element_type=F32)
    share = jnp.where(rank == (slot % CAP).astype(F32), share, 0.0)
    rows = back[...].reshape(EXPERTS * CAP, LANES)[:, :feats].astype(F32)
    mixed = jnp.dot(share, rows, precision=lax.Precision.HIGHEST, preferred_element_type=F32)
    out[...] = mixed.astype(BF16)


def hold(arrays, after):
    return pl.pallas_call(
        lambda *refs: None,
        out_shape=[shaped(a.shape, a.dtype) for a in arrays],
        in_specs=[AFTER] * (len(arrays) + len(after)),
        out_specs=[AFTER] * len(arrays),
        input_output_aliases={i: i for i in range(len(arrays))},
        compiler_params=pltpu.CompilerParams(vmem_limit_bytes=2**20),
        name="hold",
    )(*arrays, *after)


def exchange(array, axes):
    return lax.all_to_all(array, axes, split_axis=0, concat_axis=0, tiled=False)


def shift(array, axis, by):
    size = lax.axis_size(axis)
    return lax.ppermute(array, axis, [(i, (i + by) % size) for i in range(size)])


def local(queries, latents, offsets, moe_input, routes, gate_values, w_gate, w_up, w_down):
    nz, nh, nx, nl, nc = (lax.axis_size(a) for a in ("z", "h", "x", "l", "c"))
    h_at, x_at, core = (lax.axis_index(a) for a in ("h", "x", "c"))
    owners = nl * nc
    held, feats, width = w_gate.shape
    units = width // nx
    tokens = moe_input.shape[0]
    slots = held * CAP
    where_x = x_at.astype(I32).reshape(1)

    outgoing = kernel(
        functools.partial(dispatch_body, nx), "dispatch", shaped((nx * owners, slots, LANES), BF16),
        [VMEM] * 2, (routes.T, moe_input), 2**20, 2**18,
    )
    arrived = exchange(outgoing, ("x", "l", "c"))

    own = latents.shape[0] // nc
    half = lax.dynamic_slice_in_dim(latents, core * own, own, 0)
    paired = jnp.concatenate([half, shift(half, "h", 1)], axis=0)
    paired = kernel(
        pair_body, "pair", shaped((nz,) + paired.shape, BF16), [VMEM, AFTER], (paired, arrived), 2**10, 2**20
    )
    column = exchange(paired, "z")
    raw = column.reshape(nz * nh * own, WIDE)

    cut = kernel(
        cut_body, "cut", [shaped((held, feats, 2 * units), BF16)] * nx,
        [SMEM, VMEM, VMEM], (where_x, w_gate, w_up), 2**10, 2**21,
    )
    weights = [cut[0]] + [shift(cut[j], "x", j) for j in range(1, nx)]
    order = [0] + [nx - j for j in range(1, nx)]
    at_z = lax.broadcasted_iota(I32, (nz, nh, own), 0)
    at_h = (lax.broadcasted_iota(I32, (nz, nh, own), 1) + h_at) % nh
    base = ((at_z * nh + at_h) * nx * latents.shape[0] + lax.broadcasted_iota(I32, (nz, nh, own), 2)).reshape(1, -1)
    query_rows = queries.reshape(queries.shape[0] * H, WIDE)

    parts = kernel(
        functools.partial(first_body, order), "first", shaped((held * owners * CAP, 2 * units), BF16),
        [SMEM] + [VMEM] * (1 + nx) + [AFTER] * 3, (where_x, arrived, *weights, raw, query_rows, base), 2**28, 2**21,
    )
    column = raw.T
    swapped = shift(column, "c", 1)
    others = [shift(column, "x", 1), shift(column, "x", -1), shift(column, "x", 2)]
    parts = exchange(parts.reshape(nz, -1, 2 * units), "z")
    rows = parts.shape[1]
    total, rounded = kernel(
        add_body, "add", [shaped((rows, 2 * units), F32), shaped((rows, 2 * units), BF16)],
        [VMEM], (parts,), 2**18, 2**19,
    )
    added = shift(rounded, "h", 1)
    hidden, token = kernel(
        hidden_body, "hidden", [shaped((nz * nx, rows, units), BF16), shaped((8, LANES), F32)],
        [VMEM] * 2 + [AFTER] * 3, (total, added, *others[:2], swapped), 2**18, 2**20, 2**14,
    )
    hidden = exchange(hidden, ("z", "x"))
    sources = [x_at, x_at + nx - 1, x_at + 1, x_at + 2]
    spots = []
    for source in sources:
        first = (source % nx) * latents.shape[0]
        spots.append([first + core * own, first + (nc - 1 - core) * own])

    def call(which, pieces, state, last, name):
        marks = jnp.stack([offsets[0]] + [s for i in which for s in spots[i]]).astype(I32)
        both = [p for piece in pieces for p in (piece, swapped if piece is column else shift(piece, "c", 1))]
        return attend(marks, query_rows, base, both, state, last, name)

    near, far = hold(others[:2], [token])
    *state, seen = call([0, 1, 2], [column, near, far], [], False, "attend_near")
    (opposite,) = hold(others[2:], [seen])
    mixed = call([3], [opposite], state, True, "attend_far")
    result = kernel(
        functools.partial(second_body, nz, nx), "second", shaped((owners, slots, LANES), BF16),
        [VMEM] * 2 + [AFTER], (hidden, w_down, seen), 2**27, 2**21,
    )
    back = exchange(result, ("l", "c"))
    moe_output = kernel(
        combine_body, "combine", shaped((tokens, feats), BF16),
        [VMEM] * 3, (routes, gate_values, back), 2**20, 2**18,
    )

    attention_out = mixed.reshape(queries.shape[0], H * LAT)
    return (attention_out, moe_output)


def solution(mesh):
    fine = Mesh(mesh.devices.reshape(8, 2, 4, 4, 2), ("z", "h", "x", "l", "c"))
    ctx, exp = ("z", "h", "x"), ("l", "c")
    return jax.shard_map(
        local,
        mesh=fine,
        in_specs=(
            P(ctx + exp, None),
            P(ctx, None),
            P(ctx + exp),
            P(exp, ctx),
            P(exp, None),
            P(exp, None),
            P(exp, ctx, None),
            P(exp, ctx, None),
            P(exp, None, ctx),
        ),
        out_specs=(P(ctx + exp, None), P(exp, ctx)),
        check_vma=False,
    )
```

```python
import functools
import math

import jax
import jax.numpy as jnp
from jax import lax
from jax.experimental import pallas as pl
from jax.experimental.pallas import tpu as pltpu
from jax.sharding import Mesh, PartitionSpec as P

H = 128
LAT = 512
ROPE = 64
WIDE = LAT + ROPE
TOPK = 6
EXPERTS = 16
CAP = 16
LANES = 128
CLAIM = 8

SCALE_LOG2 = 192.0 ** (-0.5) * math.log2(math.e)
F32 = jnp.float32
BF16 = jnp.bfloat16
I32 = jnp.int32
VMEM = pl.BlockSpec(memory_space=pltpu.VMEM)
AFTER = pl.BlockSpec(memory_space=pl.ANY)
SMEM = pl.BlockSpec(memory_space=pltpu.SMEM)


def shaped(shape, dtype):
    return jax.ShapeDtypeStruct(shape, dtype)


def kernel(body, name, out_shape, specs, args, flops, moved, special=0):
    return pl.pallas_call(
        body,
        out_shape=out_shape,
        in_specs=specs,
        out_specs=jax.tree.map(lambda _: VMEM, out_shape),
        compiler_params=pltpu.CompilerParams(vmem_limit_bytes=(24 if special > 2**16 else 12) * 2**20),
        cost_estimate=pl.CostEstimate(flops=flops, bytes_accessed=moved, transcendentals=special),
        name=name,
    )(*args)


def attention_body(pieces, first, last, spots, queries, base, *refs):
    keys, refs = refs[:pieces], refs[pieces:]
    rows = queries.shape[0]
    row_pos = spots[0] + lax.broadcasted_iota(I32, (rows, 1), 0) // H
    query = queries[...]
    if first:
        top = jnp.full((rows, 1), -1e30, F32)
    else:
        top = refs[0][:, :1]
    scored = []
    for j, key in enumerate(keys):
        scores = jnp.dot(query, key[...], preferred_element_type=F32) * SCALE_LOG2
        scored.append(jnp.where(base[:1, :] <= row_pos - spots[1 + j], scores, -jnp.inf))
    new = top
    for scores in scored:
        new = jnp.maximum(new, jnp.max(scores, axis=1, keepdims=True))
    den, acc = 0.0, 0.0
    if not first:
        shrink = jnp.exp2(top - new)
        den, acc = refs[1][:, :1] * shrink, refs[2][...] * shrink
    for scores, key in zip(scored, keys):
        weights = jnp.exp2(scores - new)
        den = den + jnp.sum(weights, axis=1, keepdims=True)
        acc = acc + lax.dot_general(
            weights.astype(BF16), key[:LAT, :], (((1,), (1,)), ((), ())), preferred_element_type=F32
        )
    if last:
        refs[-1][...] = (acc / den).astype(BF16)
    else:
        refs[-4][...] = jnp.broadcast_to(new, (rows, LANES))
        refs[-3][...] = jnp.broadcast_to(den, (rows, LANES))
        refs[-2][...] = acc
        refs[-1][...] = jnp.zeros(refs[-1].shape, F32)


def attend(spots, queries, base, pieces, state, last, name):
    rows, count = queries.shape[0], base.shape[1] * len(pieces)
    if last:
        out = shaped((rows, LAT), BF16)
    else:
        out = [shaped((rows, LANES), F32)] * 2 + [shaped((rows, LAT), F32), shaped((8, LANES), F32)]
    body = functools.partial(attention_body, len(pieces), not state, last)
    specs = [SMEM] + [VMEM] * (2 + len(pieces) + len(state))
    args = (spots, queries, base, *pieces, *state)
    return kernel(body, name, out, specs, args, 4 * rows * count * WIDE // CLAIM, (2 * count * WIDE + 2**20) // CLAIM, rows * count // CLAIM)


def dispatch_body(copies, routes, tokens, out):
    count = tokens.shape[0]
    slot = lax.broadcasted_iota(I32, (EXPERTS * CAP, count), 0)
    named = routes[0:1, :] == slot // CAP
    for k in range(1, TOPK):
        named = named | (routes[k : k + 1, :] == slot // CAP)
    hot = named.astype(F32)
    earlier = lax.broadcasted_iota(I32, (count, count), 0) < lax.broadcasted_iota(I32, (count, count), 1)
    rank = jnp.dot(hot.astype(BF16), earlier.astype(F32).astype(BF16), preferred_element_type=F32)
    placed = jnp.where(rank == (slot % CAP).astype(F32), hot, 0.0).astype(BF16)
    sent = jnp.dot(placed, tokens[...], preferred_element_type=F32).astype(BF16)
    owners = out.shape[0] // copies
    out[...] = jnp.zeros(out.shape, BF16)
    for i in range(copies):
        out[i * owners : (i + 1) * owners, :, : tokens.shape[1]] = sent.reshape(owners, -1, tokens.shape[1])


def cut_body(spots, gate, up, *outs):
    parts = len(outs)
    units = gate.shape[2] // parts
    for j, out in enumerate(outs):
        at = pl.multiple_of(lax.rem(spots[0] + j, parts) * units, LANES)
        out[:, :, :units] = gate[:, :, pl.ds(at, units)]
        out[:, :, units:] = up[:, :, pl.ds(at, units)]


def pair_body(rows, after, out):
    for i in range(out.shape[0]):
        out[i] = rows[...]


def first_body(order, spots, arrived, *refs):
    weights, out = refs[: len(order)], refs[-1]
    held, feats = weights[0].shape[:2]
    owners = arrived.shape[0] // len(weights)
    for e in range(held):
        total = 0.0
        for j, matrix in zip(order, weights):
            at = lax.rem(spots[0] + j, len(weights)) * owners
            rows = arrived[pl.ds(at, owners), e * CAP : (e + 1) * CAP, :].reshape(owners * CAP, LANES)
            total = total + jnp.dot(rows[:, :feats], matrix[e], preferred_element_type=F32)
        out[e * owners * CAP : (e + 1) * owners * CAP, :] = total.astype(BF16)


def add_body(parts, total, rounded):
    sums = parts[0].astype(F32)
    for i in range(1, parts.shape[0]):
        sums = sums + parts[i].astype(F32)
    total[...] = sums
    rounded[...] = sums.astype(BF16)


def hidden_body(total, other, *refs):
    out, token = refs[-2:]
    sums = total[...] + other[...].astype(F32)
    units = sums.shape[1] // 2
    gate = sums[:, :units]
    hidden = (gate / (1.0 + jnp.exp(-gate)) * sums[:, units:]).astype(BF16)
    for i in range(out.shape[0]):
        out[i] = hidden
    token[...] = jnp.zeros(token.shape, F32)


def second_body(deep, across, hidden, down, *refs):
    out = refs[-1]
    held, feats = down.shape[0], down.shape[2]
    units = hidden.shape[2]
    group = deep // held
    owners = out.shape[0]
    out[...] = jnp.zeros(out.shape, BF16)
    for e in range(held):
        total = 0.0
        for x in range(across):
            rows = jnp.concatenate([hidden[(group * e + i) * across + x] for i in range(group)], axis=0)
            total = total + jnp.dot(rows, down[e, x * units : (x + 1) * units, :], preferred_element_type=F32)
        out[:, e * CAP : (e + 1) * CAP, :feats] = total.astype(BF16).reshape(owners, CAP, feats)


def combine_body(routes, gates, back, out):
    count, feats = out.shape
    slot = lax.broadcasted_iota(I32, (count, EXPERTS * CAP), 1)
    hot = jnp.zeros(slot.shape, F32)
    share = jnp.zeros(slot.shape, F32)
    for k in range(TOPK):
        here = routes[:, k : k + 1] == slot // CAP
        hot = jnp.where(here, 1.0, hot)
        share = share + jnp.where(here, gates[:, k : k + 1], 0.0)
    earlier = lax.broadcasted_iota(I32, (count, count), 1) < lax.broadcasted_iota(I32, (count, count), 0)
    rank = jnp.dot(earlier.astype(F32).astype(BF16), hot.astype(BF16), preferred_element_type=F32)
    share = jnp.where(rank == (slot % CAP).astype(F32), share, 0.0)
    rows = back[...].reshape(EXPERTS * CAP, LANES)[:, :feats].astype(F32)
    mixed = jnp.dot(share, rows, precision=lax.Precision.HIGHEST, preferred_element_type=F32)
    out[...] = mixed.astype(BF16)


def hold(arrays, after):
    return pl.pallas_call(
        lambda *refs: None,
        out_shape=[shaped(a.shape, a.dtype) for a in arrays],
        in_specs=[AFTER] * (len(arrays) + len(after)),
        out_specs=[AFTER] * len(arrays),
        input_output_aliases={i: i for i in range(len(arrays))},
        compiler_params=pltpu.CompilerParams(vmem_limit_bytes=2**20),
        name="hold",
    )(*arrays, *after)


def exchange(array, axes):
    return lax.all_to_all(array, axes, split_axis=0, concat_axis=0, tiled=False)


def shift(array, axis, by):
    size = lax.axis_size(axis)
    return lax.ppermute(array, axis, [(i, (i + by) % size) for i in range(size)])


def local(queries, latents, offsets, moe_input, routes, gate_values, w_gate, w_up, w_down):
    nz, nh, nx, nl, nc = (lax.axis_size(a) for a in ("z", "h", "x", "l", "c"))
    h_at, x_at, core = (lax.axis_index(a) for a in ("h", "x", "c"))
    owners = nl * nc
    held, feats, width = w_gate.shape
    units = width // nx
    tokens = moe_input.shape[0]
    slots = held * CAP
    where_x = x_at.astype(I32).reshape(1)

    outgoing = kernel(
        functools.partial(dispatch_body, nx), "dispatch", shaped((nx * owners, slots, LANES), BF16),
        [VMEM] * 2, (routes.T, moe_input), 2**20, 2**18,
    )
    arrived = exchange(outgoing, ("x", "l", "c"))

    own = latents.shape[0] // nc
    half = lax.dynamic_slice_in_dim(latents, core * own, own, 0)
    paired = jnp.concatenate([half, shift(half, "h", 1)], axis=0)
    paired = kernel(
        pair_body, "pair", shaped((nz,) + paired.shape, BF16), [VMEM, AFTER], (paired, arrived), 2**10, 2**20
    )
    column = exchange(paired, "z")
    raw = column.reshape(nz * nh * own, WIDE)

    cut = kernel(
        cut_body, "cut", [shaped((held, feats, 2 * units), BF16)] * nx,
        [SMEM, VMEM, VMEM], (where_x, w_gate, w_up), 2**10, 2**21,
    )
    weights = [cut[0]] + [shift(cut[j], "x", j) for j in range(1, nx)]
    order = [0] + [nx - j for j in range(1, nx)]
    at_z = lax.broadcasted_iota(I32, (nz, nh, own), 0)
    at_h = (lax.broadcasted_iota(I32, (nz, nh, own), 1) + h_at) % nh
    base = ((at_z * nh + at_h) * nx * latents.shape[0] + lax.broadcasted_iota(I32, (nz, nh, own), 2)).reshape(1, -1)
    query_rows = queries.reshape(queries.shape[0] * H, WIDE)

    parts = kernel(
        functools.partial(first_body, order), "first", shaped((held * owners * CAP, 2 * units), BF16),
        [SMEM] + [VMEM] * (1 + nx) + [AFTER] * 3, (where_x, arrived, *weights, raw, query_rows, base), 2**28, 2**21,
    )
    column = raw.T
    swapped = shift(column, "c", 1)
    others = [shift(column, "x", 1), shift(column, "x", -1), shift(column, "x", 2)]
    parts = exchange(parts.reshape(nz, -1, 2 * units), "z")
    rows = parts.shape[1]
    total, rounded = kernel(
        add_body, "add", [shaped((rows, 2 * units), F32), shaped((rows, 2 * units), BF16)],
        [VMEM], (parts,), 2**18, 2**19,
    )
    added = shift(rounded, "h", 1)
    sources = [x_at, x_at + nx - 1, x_at + 1, x_at + 2]
    spots = []
    for source in sources:
        first = (source % nx) * latents.shape[0]
        spots.append([first + core * own, first + (nc - 1 - core) * own])

    def call(which, pieces, state, last, name):
        marks = jnp.stack([offsets[0]] + [s for i in which for s in spots[i]]).astype(I32)
        both = [p for piece in pieces for p in (piece, swapped if piece is column else shift(piece, "c", 1))]
        return attend(marks, query_rows, base, both, state, last, name)

    *state, seen = call([0], [column], [], False, "attend_own")
    near, far, opposite = hold(others, [added, seen])
    hidden, token = kernel(
        hidden_body, "hidden", [shaped((nz * nx, rows, units), BF16), shaped((8, LANES), F32)],
        [VMEM] * 2 + [AFTER] * 2, (total, added, opposite, seen), 2**18, 2**20, 2**14,
    )
    near, far, opposite = hold([near, far, opposite], [token])
    *state, seen = call([1, 2], [near, far], state, False, "attend_near")
    mixed = call([3], [opposite], state, True, "attend_far")
    hidden = exchange(hidden, ("z", "x"))
    result = kernel(
        functools.partial(second_body, nz, nx), "second", shaped((owners, slots, LANES), BF16),
        [VMEM] * 2 + [AFTER], (hidden, w_down, seen), 2**27, 2**21,
    )
    back = exchange(result, ("l", "c"))
    moe_output = kernel(
        combine_body, "combine", shaped((tokens, feats), BF16),
        [VMEM] * 3, (routes, gate_values, back), 2**20, 2**18,
    )

    attention_out = mixed.reshape(queries.shape[0], H * LAT)
    return (attention_out, moe_output)


def solution(mesh):
    fine = Mesh(mesh.devices.reshape(8, 2, 4, 4, 2), ("z", "h", "x", "l", "c"))
    ctx, exp = ("z", "h", "x"), ("l", "c")
    return jax.shard_map(
        local,
        mesh=fine,
        in_specs=(
            P(ctx + exp, None),
            P(ctx, None),
            P(ctx + exp),
            P(exp, ctx),
            P(exp, None),
            P(exp, None),
            P(exp, ctx, None),
            P(exp, ctx, None),
            P(exp, None, ctx),
        ),
        out_specs=(P(ctx + exp, None), P(exp, ctx)),
        check_vma=False,
    )
```

```python
import functools
import math

import jax
import jax.numpy as jnp
from jax import lax
from jax.experimental import pallas as pl
from jax.experimental.pallas import tpu as pltpu
from jax.sharding import Mesh, PartitionSpec as P

H = 128
LAT = 512
ROPE = 64
WIDE = LAT + ROPE
TOPK = 6
EXPERTS = 16
CAP = 16
LANES = 128
CLAIM = 8

SCALE_LOG2 = 192.0 ** (-0.5) * math.log2(math.e)
F32 = jnp.float32
BF16 = jnp.bfloat16
I32 = jnp.int32
VMEM = pl.BlockSpec(memory_space=pltpu.VMEM)
AFTER = pl.BlockSpec(memory_space=pl.ANY)
SMEM = pl.BlockSpec(memory_space=pltpu.SMEM)


def shaped(shape, dtype):
    return jax.ShapeDtypeStruct(shape, dtype)


def kernel(body, name, out_shape, specs, args, flops, moved, special=0):
    return pl.pallas_call(
        body,
        out_shape=out_shape,
        in_specs=specs,
        out_specs=jax.tree.map(lambda _: VMEM, out_shape),
        compiler_params=pltpu.CompilerParams(vmem_limit_bytes=(24 if special > 2**16 else 12) * 2**20),
        cost_estimate=pl.CostEstimate(flops=flops, bytes_accessed=moved, transcendentals=special),
        name=name,
    )(*args)


def attention_body(pieces, first, last, spots, queries, base, *refs):
    keys, refs = refs[:pieces], refs[pieces:]
    rows = queries.shape[0]
    row_pos = spots[0] + lax.broadcasted_iota(I32, (rows, 1), 0) // H
    query = queries[...]
    if first:
        top = jnp.full((rows, 1), -1e30, F32)
    else:
        top = refs[0][:, :1]
    scored = []
    for j, key in enumerate(keys):
        scores = jnp.dot(query, key[...], preferred_element_type=F32) * SCALE_LOG2
        scored.append(jnp.where(base[:1, :] <= row_pos - spots[1 + j], scores, -jnp.inf))
    new = top
    for scores in scored:
        new = jnp.maximum(new, jnp.max(scores, axis=1, keepdims=True))
    den, acc = 0.0, 0.0
    if not first:
        shrink = jnp.exp2(top - new)
        den, acc = refs[1][:, :1] * shrink, refs[2][...] * shrink
    for scores, key in zip(scored, keys):
        weights = jnp.exp2(scores - new)
        den = den + jnp.sum(weights, axis=1, keepdims=True)
        acc = acc + lax.dot_general(
            weights.astype(BF16), key[:LAT, :], (((1,), (1,)), ((), ())), preferred_element_type=F32
        )
    if last:
        refs[-1][...] = (acc / den).astype(BF16)
    else:
        refs[-4][...] = jnp.broadcast_to(new, (rows, LANES))
        refs[-3][...] = jnp.broadcast_to(den, (rows, LANES))
        refs[-2][...] = acc
        refs[-1][...] = jnp.zeros(refs[-1].shape, F32)


def attend(spots, queries, base, pieces, state, last, name):
    rows, count = queries.shape[0], base.shape[1] * len(pieces)
    if last:
        out = shaped((rows, LAT), BF16)
    else:
        out = [shaped((rows, LANES), F32)] * 2 + [shaped((rows, LAT), F32), shaped((8, LANES), F32)]
    body = functools.partial(attention_body, len(pieces), not state, last)
    specs = [SMEM] + [VMEM] * (2 + len(pieces) + len(state))
    args = (spots, queries, base, *pieces, *state)
    return kernel(body, name, out, specs, args, 4 * rows * count * WIDE // CLAIM, (2 * count * WIDE + 2**20) // CLAIM, rows * count // CLAIM)


def dispatch_body(copies, routes, tokens, out):
    count = tokens.shape[0]
    slot = lax.broadcasted_iota(I32, (EXPERTS * CAP, count), 0)
    named = routes[0:1, :] == slot // CAP
    for k in range(1, TOPK):
        named = named | (routes[k : k + 1, :] == slot // CAP)
    hot = named.astype(F32)
    earlier = lax.broadcasted_iota(I32, (count, count), 0) < lax.broadcasted_iota(I32, (count, count), 1)
    rank = jnp.dot(hot.astype(BF16), earlier.astype(F32).astype(BF16), preferred_element_type=F32)
    placed = jnp.where(rank == (slot % CAP).astype(F32), hot, 0.0).astype(BF16)
    sent = jnp.dot(placed, tokens[...], preferred_element_type=F32).astype(BF16)
    owners = out.shape[0] // copies
    out[...] = jnp.zeros(out.shape, BF16)
    for i in range(copies):
        out[i * owners : (i + 1) * owners, :, : tokens.shape[1]] = sent.reshape(owners, -1, tokens.shape[1])


def cut_body(spots, gate, up, *outs):
    parts = len(outs)
    units = gate.shape[2] // parts
    for j, out in enumerate(outs):
        at = pl.multiple_of(lax.rem(spots[0] + j, parts) * units, LANES)
        out[:, :, :units] = gate[:, :, pl.ds(at, units)]
        out[:, :, units:] = up[:, :, pl.ds(at, units)]


def pair_body(rows, after, out):
    for i in range(out.shape[0]):
        out[i] = rows[...]


def first_body(order, spots, arrived, *refs):
    weights, out = refs[: len(order)], refs[-1]
    held, feats = weights[0].shape[:2]
    owners = arrived.shape[0] // len(weights)
    for e in range(held):
        total = 0.0
        for j, matrix in zip(order, weights):
            at = lax.rem(spots[0] + j, len(weights)) * owners
            rows = arrived[pl.ds(at, owners), e * CAP : (e + 1) * CAP, :].reshape(owners * CAP, LANES)
            total = total + jnp.dot(rows[:, :feats], matrix[e], preferred_element_type=F32)
        out[e * owners * CAP : (e + 1) * owners * CAP, :] = total.astype(BF16)


def add_body(parts, total, rounded):
    sums = parts[0].astype(F32)
    for i in range(1, parts.shape[0]):
        sums = sums + parts[i].astype(F32)
    total[...] = sums
    rounded[...] = sums.astype(BF16)


def hidden_body(total, other, *refs):
    out, token = refs[-2:]
    sums = total[...] + other[...].astype(F32)
    units = sums.shape[1] // 2
    gate = sums[:, :units]
    hidden = (gate / (1.0 + jnp.exp(-gate)) * sums[:, units:]).astype(BF16)
    for i in range(out.shape[0]):
        out[i] = hidden
    token[...] = jnp.zeros(token.shape, F32)


def second_body(deep, across, hidden, down, out):
    held, feats = down.shape[0], down.shape[2]
    units = hidden.shape[2]
    group = deep // held
    owners = out.shape[0]
    out[...] = jnp.zeros(out.shape, BF16)
    for e in range(held):
        total = 0.0
        for x in range(across):
            rows = jnp.concatenate([hidden[(group * e + i) * across + x] for i in range(group)], axis=0)
            total = total + jnp.dot(rows, down[e, x * units : (x + 1) * units, :], preferred_element_type=F32)
        out[:, e * CAP : (e + 1) * CAP, :feats] = total.astype(BF16).reshape(owners, CAP, feats)


def combine_body(routes, gates, back, out):
    count, feats = out.shape
    slot = lax.broadcasted_iota(I32, (count, EXPERTS * CAP), 1)
    hot = jnp.zeros(slot.shape, F32)
    share = jnp.zeros(slot.shape, F32)
    for k in range(TOPK):
        here = routes[:, k : k + 1] == slot // CAP
        hot = jnp.where(here, 1.0, hot)
        share = share + jnp.where(here, gates[:, k : k + 1], 0.0)
    earlier = lax.broadcasted_iota(I32, (count, count), 1) < lax.broadcasted_iota(I32, (count, count), 0)
    rank = jnp.dot(earlier.astype(F32).astype(BF16), hot.astype(BF16), preferred_element_type=F32)
    share = jnp.where(rank == (slot % CAP).astype(F32), share, 0.0)
    rows = back[...].reshape(EXPERTS * CAP, LANES)[:, :feats].astype(F32)
    mixed = jnp.dot(share, rows, precision=lax.Precision.HIGHEST, preferred_element_type=F32)
    out[...] = mixed.astype(BF16)


def hold(arrays, after):
    return pl.pallas_call(
        lambda *refs: None,
        out_shape=[shaped(a.shape, a.dtype) for a in arrays],
        in_specs=[AFTER] * (len(arrays) + len(after)),
        out_specs=[AFTER] * len(arrays),
        input_output_aliases={i: i for i in range(len(arrays))},
        compiler_params=pltpu.CompilerParams(vmem_limit_bytes=2**20),
        name="hold",
    )(*arrays, *after)


def exchange(array, axes):
    return lax.all_to_all(array, axes, split_axis=0, concat_axis=0, tiled=False)


def shift(array, axis, by):
    size = lax.axis_size(axis)
    return lax.ppermute(array, axis, [(i, (i + by) % size) for i in range(size)])


def local(queries, latents, offsets, moe_input, routes, gate_values, w_gate, w_up, w_down):
    nz, nh, nx, nl, nc = (lax.axis_size(a) for a in ("z", "h", "x", "l", "c"))
    h_at, x_at, core = (lax.axis_index(a) for a in ("h", "x", "c"))
    owners = nl * nc
    held, feats, width = w_gate.shape
    units = width // nx
    tokens = moe_input.shape[0]
    slots = held * CAP
    where_x = x_at.astype(I32).reshape(1)

    outgoing = kernel(
        functools.partial(dispatch_body, nx), "dispatch", shaped((nx * owners, slots, LANES), BF16),
        [VMEM] * 2, (routes.T, moe_input), 2**20, 2**18,
    )
    arrived = exchange(outgoing, ("x", "l", "c"))

    own = latents.shape[0] // nc
    half = lax.dynamic_slice_in_dim(latents, core * own, own, 0)
    paired = jnp.concatenate([half, shift(half, "h", 1)], axis=0)
    paired = kernel(
        pair_body, "pair", shaped((nz,) + paired.shape, BF16), [VMEM, AFTER], (paired, arrived), 2**10, 2**20
    )
    column = exchange(paired, "z")
    raw = column.reshape(nz * nh * own, WIDE)

    cut = kernel(
        cut_body, "cut", [shaped((held, feats, 2 * units), BF16)] * nx,
        [SMEM, VMEM, VMEM], (where_x, w_gate, w_up), 2**10, 2**21,
    )
    weights = [cut[0]] + [shift(cut[j], "x", j) for j in range(1, nx)]
    order = [0] + [nx - j for j in range(1, nx)]
    at_z = lax.broadcasted_iota(I32, (nz, nh, own), 0)
    at_h = (lax.broadcasted_iota(I32, (nz, nh, own), 1) + h_at) % nh
    base = ((at_z * nh + at_h) * nx * latents.shape[0] + lax.broadcasted_iota(I32, (nz, nh, own), 2)).reshape(1, -1)
    query_rows = queries.reshape(queries.shape[0] * H, WIDE)

    parts = kernel(
        functools.partial(first_body, order), "first", shaped((held * owners * CAP, 2 * units), BF16),
        [SMEM] + [VMEM] * (1 + nx) + [AFTER] * 3, (where_x, arrived, *weights, raw, query_rows, base), 2**28, 2**21,
    )
    column = raw.T
    others = [shift(column, "x", 1), shift(column, "x", -1), shift(column, "x", 2)]
    parts = exchange(parts.reshape(nz, -1, 2 * units), "z")
    rows = parts.shape[1]
    total, rounded = kernel(
        add_body, "add", [shaped((rows, 2 * units), F32), shaped((rows, 2 * units), BF16)],
        [VMEM], (parts,), 2**18, 2**19,
    )
    added = shift(rounded, "h", 1)
    hidden, token = kernel(
        hidden_body, "hidden", [shaped((nz * nx, rows, units), BF16), shaped((8, LANES), F32)],
        [VMEM] * 2 + [AFTER] * 2, (total, added, *others[:2]), 2**18, 2**20, 2**14,
    )
    hidden = exchange(hidden, ("z", "x"))
    result = kernel(
        functools.partial(second_body, nz, nx), "second", shaped((owners, slots, LANES), BF16),
        [VMEM] * 2, (hidden, w_down), 2**27, 2**21,
    )
    back = exchange(result, ("l", "c"))
    moe_output = kernel(
        combine_body, "combine", shaped((tokens, feats), BF16),
        [VMEM] * 3, (routes, gate_values, back), 2**20, 2**18,
    )

    sources = [x_at, x_at + nx - 1, x_at + 1, x_at + 2]
    spots = []
    for source in sources:
        first = (source % nx) * latents.shape[0]
        spots.append([first + core * own, first + (nc - 1 - core) * own])

    def call(which, pieces, state, last, name):
        marks = jnp.stack([offsets[0]] + [s for i in which for s in spots[i]]).astype(I32)
        both = [p for piece in pieces for p in (piece, shift(piece, "c", 1))]
        return attend(marks, query_rows, base, both, state, last, name)

    *state, seen = call([0, 1, 2], [column, *hold(others[:2], [token])], [], False, "attend_near")
    mixed = call([3], hold(others[2:], [token, seen]), state, True, "attend_far")
    attention_out = mixed.reshape(queries.shape[0], H * LAT)
    return (attention_out, moe_output)


def solution(mesh):
    fine = Mesh(mesh.devices.reshape(8, 2, 4, 4, 2), ("z", "h", "x", "l", "c"))
    ctx, exp = ("z", "h", "x"), ("l", "c")
    return jax.shard_map(
        local,
        mesh=fine,
        in_specs=(
            P(ctx + exp, None),
            P(ctx, None),
            P(ctx + exp),
            P(exp, ctx),
            P(exp, None),
            P(exp, None),
            P(exp, ctx, None),
            P(exp, ctx, None),
            P(exp, None, ctx),
        ),
        out_specs=(P(ctx + exp, None), P(exp, ctx)),
        check_vma=False,
    )
```
